128 devices in a mesh: tm: 8 (over x, core), sy: 4 (over z), sx: 4 (over y).
Axes of the slice: x: 4, y: 4, z: 4, core: 2. Of those that a mesh axis runs over, the one named last changes fastest.
Arguments:
- latent_init: float32 [64, 96, 320], P('sy', 'sx'), may hold values from -80 to 80
- step_noise: bfloat16 [32, 64, 96, 320], P('tm', 'sy', 'sx'), may hold values from -6 to 6
- coef_state: float32 [32], P('tm'), may hold values from -0.06 to -0.01
- coef_drift: float32 [32], P('tm'), may hold values from -0.1 to 0.1
- coef_noise: float32 [32], P('tm'), may hold values from 0.05 to 0.2
- step_index: int32 [32], P('tm'), may hold values from 0 to 999
- time_table: float32 [1000, 320], replicated, may hold values from -1.5 to 1.5
- norm_gain: float32 [320], replicated, may hold values from 0.25 to 1.75
- conv_weight: bfloat16 [3, 3, 320, 320], replicated, may hold values from -0.109375 to 0.109375
- reward_grad: float32 [64, 96, 320], P('sy', 'sx'), may hold values from -0.18 to 0.18
Outputs:
- trajectory: float32 [32, 64, 96, 320], P('tm', 'sy', 'sx')
- grad_weight: float32 [3, 3, 320, 320], P(None, None, None, 'tm')
The draws below stay inside these ranges and needn't reach their ends.
All inputs are finite; a program needn't handle non-finite values.
Results may differ from the reference program's by a relative error of at most 0.0009.
The reference program's roundings to bfloat16 on the way (of `activation` and `up_half`) count: a program that leaves them out, or rounds other values in their place, can miss the bound.
Values may be sent and summed in bfloat16 or wider, within the bound.
A program may use at most 128 MiB of HBM per device.

```python
import math
import jax
import jax.numpy as jnp
from jax import lax

CH = 320
GROUPS = 32
TABLE = 1000
ITERS = 2
TSTEP = 32
LAT_H = 64
LAT_W = 96


def draw_latent_init(key, part):
    k_base, k_rows, k_cols, k_chan = jax.random.split(key, 4)
    full_shape = (LAT_H, LAT_W, CH)
    row_pos = jnp.arange(LAT_H, dtype=jnp.float32) / max(LAT_H - 1, 1)
    col_pos = jnp.arange(LAT_W, dtype=jnp.float32) / max(LAT_W - 1, 1)
    row_scale = jnp.exp(math.log(3.0) * (row_pos - 0.5)) * jnp.exp(jax.random.uniform(k_rows, (LAT_H,), jnp.float32, -0.35, 0.35))
    col_scale = jnp.exp(math.log(3.0) * (col_pos - 0.5)) * jnp.exp(jax.random.uniform(k_cols, (LAT_W,), jnp.float32, -0.35, 0.35))
    chan_scale = jnp.exp(jax.random.uniform(k_chan, (CH,), jnp.float32, math.log(0.3), math.log(3.0)))
    base_draw = jnp.clip(jax.random.normal(k_base, full_shape, jnp.float32), -4.0, 4.0)
    return base_draw * row_scale[:, None, None] * col_scale[None, :, None] * chan_scale[None, None, :]


def touch_ends(drawn, key, low, top_value):
    longest = drawn.shape.index(max(drawn.shape))
    spots = []
    for shift in (0, 1):
        where = [jax.random.randint(jax.random.fold_in(key, axis), (), 0, length) for axis, length in enumerate(drawn.shape)]
        where[longest] = (where[longest] + shift) % drawn.shape[longest]
        spots.append(tuple(where))
    return drawn.at[spots[0]].set(low).at[spots[1]].set(top_value)


def block_scale(own_key, dims, cuts, smallest, top_value):
    gain = 1.0
    for dim, parts in cuts:
        draws = jax.random.uniform(jax.random.fold_in(jax.random.fold_in(own_key, 6), dim), (parts,), jnp.float32, smallest / len(cuts), top_value / len(cuts))
        gain = gain * jnp.repeat(jnp.exp(draws), dims[dim] // parts).reshape((-1,) + (1,) * (len(dims) - 1 - dim))
    return gain


def normal_values(key, extent, width, limit, cuts=(), kind=jnp.bfloat16):
    values = width * jax.random.normal(key, extent, jnp.float32)
    if cuts:
        values = values * block_scale(key, extent, cuts, -0.22, 0.18)
    return jnp.clip(values, -limit, limit).astype(kind)


def setup_inputs(seed: int = 0) -> dict:
    seeds = jax.random.split(jax.random.key(seed), 11)
    latent_init = draw_latent_init(jax.random.fold_in(seeds[10], 71), 0)
    step_noise = normal_values(seeds[1], (TSTEP, LAT_H, LAT_W, CH), 1.0, 6.0, ((0, 8), (1, 4), (2, 4)))
    coef_state = jnp.clip(-0.06 + 0.04999999888241291 * jax.random.uniform(seeds[2], (TSTEP,), jnp.float32) ** block_scale(seeds[2], (TSTEP,), ((0, 8),), -0.2, 0.2), -0.06, -0.01)
    coef_drift = jnp.clip(jax.random.uniform(seeds[3], (TSTEP,), jnp.float32, -0.1, 0.1) * block_scale(seeds[3], (TSTEP,), ((0, 8),), -0.4, 0.0), -0.1, 0.1)
    coef_noise = jnp.clip(jnp.exp(math.log(0.2) - 1.3862944 * jax.random.uniform(seeds[4], (TSTEP,), jnp.float32) ** block_scale(seeds[4], (TSTEP,), ((0, 8),), -0.2, 0.2)), 0.05, 0.2)
    step_index = touch_ends(jax.random.randint(seeds[5], (TSTEP,), 0, TABLE), jax.random.fold_in(seeds[5], 1), 0, TABLE - 1).astype(jnp.int32)
    time_table = normal_values(seeds[6], (TABLE, CH), 0.3, 1.5, (), jnp.float32)
    norm_gain = jnp.clip(1.0 + 0.15 * jax.random.normal(seeds[7], (CH,), jnp.float32), 0.25, 1.75)
    conv_weight = normal_values(seeds[8], (3, 3, CH, CH), (9 * CH) ** -0.5, 0.109375)
    reward_grad = normal_values(seeds[9], (LAT_H, LAT_W, CH), 0.03, 0.18, ((0, 4), (1, 4)), jnp.float32)
    return dict(latent_init=latent_init, step_noise=step_noise, coef_state=coef_state, coef_drift=coef_drift, coef_noise=coef_noise, step_index=step_index, time_table=time_table, norm_gain=norm_gain, conv_weight=conv_weight, reward_grad=reward_grad)


EPSILON = 1e-05

def prepare_one(one_field, modulate):
    grouped = one_field.reshape(LAT_H * LAT_W, GROUPS, CH // GROUPS)
    cell_count = LAT_H * LAT_W * (CH // GROUPS)
    center = lax.optimization_barrier(jnp.sum(grouped, axis=(0, 2))) / cell_count
    shifted = grouped - center[None, :, None]
    spread = lax.optimization_barrier(jnp.sum(shifted * shifted, axis=(0, 2))) / cell_count
    inv_std = 1.0 / jnp.sqrt(spread + EPSILON)
    normal_field = (shifted * inv_std[None, :, None]).reshape(one_field.shape)
    pre_act = normal_field * modulate[None, None, :]
    activation = jax.nn.silu(pre_act).astype(jnp.bfloat16)
    act_pad = jnp.pad(activation, ((1, 1), (1, 1), (0, 0)))
    return (normal_field, inv_std, pre_act, act_pad)

def convolve_one(act_pad, conv_weight):
    result = jnp.zeros((LAT_H * LAT_W, CH), jnp.float32)
    for row_off in range(3):
        for col_off in range(3):
            window = act_pad[row_off:row_off + LAT_H, col_off:col_off + LAT_W, :].reshape(LAT_H * LAT_W, CH)
            result = result + jnp.dot(window, conv_weight[row_off, col_off], preferred_element_type=jnp.float32)
    return result.reshape(LAT_H, LAT_W, CH)

def drift_all(states, modulation, conv_weight):

    def map_one(field_pair):
        one_field, modulate = field_pair
        act_cache = prepare_one(one_field, modulate)
        return one_field + convolve_one(act_cache[3], conv_weight)
    return lax.map(map_one, (states, modulation))

def backprop_one(one_field, modulate, upstream, conv_weight, need_state):
    normal_field, inv_std, pre_act, act_pad = prepare_one(one_field, modulate)
    up_half = upstream.astype(jnp.bfloat16)
    up_flat = up_half.reshape(LAT_H * LAT_W, CH)
    pieces = []
    for row_off in range(3):
        row_terms = []
        for col_off in range(3):
            window = act_pad[row_off:row_off + LAT_H, col_off:col_off + LAT_W, :].reshape(LAT_H * LAT_W, CH)
            row_terms.append(jnp.dot(window.T, up_flat, preferred_element_type=jnp.float32))
        pieces.append(jnp.stack(row_terms))
    grad_piece = jnp.stack(pieces)
    if not need_state:
        return (jnp.zeros_like(upstream), grad_piece)
    up_pad = jnp.pad(up_half, ((1, 1), (1, 1), (0, 0)))
    d_act = jnp.zeros((LAT_H * LAT_W, CH), jnp.float32)
    for row_off in range(3):
        for col_off in range(3):
            window = up_pad[2 - row_off:2 - row_off + LAT_H, 2 - col_off:2 - col_off + LAT_W, :].reshape(LAT_H * LAT_W, CH)
            d_act = d_act + jnp.dot(window, conv_weight[row_off, col_off].T, preferred_element_type=jnp.float32)
    d_act = d_act.reshape(LAT_H, LAT_W, CH)
    sig_value = jax.nn.sigmoid(pre_act)
    d_norm = d_act * sig_value * (1.0 + pre_act * (1.0 - sig_value)) * modulate[None, None, :]
    cell_count = LAT_H * LAT_W * (CH // GROUPS)
    grouped_d = d_norm.reshape(LAT_H * LAT_W, GROUPS, CH // GROUPS)
    grouped_n = normal_field.reshape(LAT_H * LAT_W, GROUPS, CH // GROUPS)
    plain_mean = lax.optimization_barrier(jnp.sum(grouped_d, axis=(0, 2))) / cell_count
    cross_mean = lax.optimization_barrier(jnp.sum(grouped_d * grouped_n, axis=(0, 2))) / cell_count
    d_group = (grouped_d - plain_mean[None, :, None] - grouped_n * cross_mean[None, :, None]) * inv_std[None, :, None]
    return (upstream + d_group.reshape(upstream.shape), grad_piece)

def reference(latent_init, step_noise, coef_state, coef_drift, coef_noise, step_index, time_table, norm_gain, conv_weight, reward_grad):
    modulation = norm_gain[None, :] * (1.0 + time_table[step_index])
    state_c = coef_state[:, None, None, None]
    drift_c = coef_drift[:, None, None, None]
    noise_c = coef_noise[:, None, None, None]
    states = jnp.broadcast_to(latent_init[None], (TSTEP, LAT_H, LAT_W, CH))
    saved_states = []
    trajectory = states
    for sweep_index in range(ITERS):
        saved_states.append(states)
        drift_term = drift_all(states, modulation, conv_weight)
        increment = state_c * states + drift_c * drift_term + noise_c * step_noise.astype(jnp.float32)
        running = jnp.cumsum(increment, axis=0)
        trajectory = latent_init[None] + running
        before = jnp.concatenate([jnp.zeros_like(running[:1]), running[:-1]], axis=0)
        states = latent_init[None] + before
    adjoint = jnp.broadcast_to(reward_grad[None], trajectory.shape)
    grad_total = jnp.zeros((3, 3, CH, CH), jnp.float32)
    for sweep_index in range(ITERS - 1, -1, -1):
        upstream = drift_c * adjoint
        need_state = sweep_index > 0

        def scan_step(carry_sum, scan_items, need_state=need_state):
            one_field, modulate, one_up = scan_items
            d_state, grad_piece = backprop_one(one_field, modulate, one_up, conv_weight, need_state)
            return (carry_sum + grad_piece, d_state)
        grad_total, d_states = lax.scan(scan_step, grad_total, (saved_states[sweep_index], modulation, upstream))
        if need_state:
            through = state_c * adjoint + d_states
            suffix = jnp.cumsum(through[::-1], axis=0)[::-1]
            adjoint = jnp.concatenate([suffix[1:], jnp.zeros_like(suffix[:1])], axis=0)
    return (trajectory, grad_total)
```

```python
import functools
import itertools

import jax
import jax.numpy as jnp
from jax import lax
from jax.experimental import pallas as pl
from jax.experimental.pallas import tpu as pltpu
from jax.sharding import PartitionSpec as P

MESH = pl.DeviceIdType.MESH
VM = pl.BlockSpec(memory_space=pltpu.VMEM)
SM = pl.BlockSpec(memory_space=pltpu.SMEM)
F32 = jnp.float32
BF16 = jnp.bfloat16
HI = lax.Precision.HIGHEST
EPSILON = 1e-05
GSIZE = 10
T = 4
H = 16
W = 24
C = 320
PW = 32
HP = H + 2
AW = 1024
VLIM = 60 << 20


def rcopy(src, dst, ssem, rsem, dev):
    return pltpu.make_async_remote_copy(
        src_ref=src, dst_ref=dst, send_sem=ssem, recv_sem=rsem, device_id=dev, device_id_type=MESH
    )


def greet(devs):
    sem = pltpu.get_barrier_semaphore()
    for dev in devs:
        pl.semaphore_signal(sem, inc=1, device_id=dev, device_id_type=MESH)
    pl.semaphore_wait(sem, len(devs))


class Where:
    def __init__(self, dims):
        self.nt, self.ny, self.nx = dims
        self.tm = lax.axis_index("tm")
        self.y = lax.axis_index("sy")
        self.x = lax.axis_index("sx")
        self.nd = self.ny * self.nx
        self.me = self.y * self.nx + self.x

    def dev(self, tm, y, x):
        return (tm, y, x)

    def tile(self, d):
        q = lax.rem(self.me + d, self.nd)
        return q, self.dev(self.tm, lax.div(q, self.nx), lax.rem(q, self.nx))

    def shift(self, dy, dx):
        return self.dev(
            self.tm,
            lax.rem(self.y + dy + self.ny, self.ny),
            lax.rem(self.x + dx + self.nx, self.nx),
        )

    def tiles(self):
        return [self.tile(d)[1] for d in range(1, self.nd)]

    def line(self):
        c = lax.rem(self.tm, 2)
        return [
            self.dev(self.tm + 1 - 2 * c, self.y, self.x),
            self.dev(lax.rem(self.tm + 2, self.nt), self.y, self.x),
            self.dev(lax.rem(self.tm + self.nt - 2, self.nt), self.y, self.x),
        ]


def gather_start(w, buf, ssem, rsem):
    out = []
    for d in range(1, w.nd):
        _, dev = w.tile(d)
        cp = rcopy(buf.at[w.me], buf.at[w.me], ssem.at[d], rsem.at[w.me], dev)
        cp.start()
        out.append(cp)
    return out


def gather_wait(w, buf, ssem, rsem, sent):
    for cp in sent:
        cp.wait_send()
    for d in range(1, w.nd):
        q, dev = w.tile(d)
        rcopy(buf.at[q], buf.at[q], ssem.at[d], rsem.at[q], dev).wait_recv()


def group_matrix():
    row = lax.broadcasted_iota(jnp.int32, (C, C), 0)
    col = lax.broadcasted_iota(jnp.int32, (C, C), 1)
    same = ((row * 6554) >> 16) == ((col * 6554) >> 16)
    return same.astype(F32)


def moments(buf, w):
    gm = group_matrix()
    n = float(H * W)
    both = buf[...]
    mean = jnp.sum(both[:, 0:T], axis=0) * (1.0 / w.nd)
    center = jnp.dot(mean, gm, precision=HI, preferred_element_type=F32) * (1.0 / GSIZE)
    off = both[:, 0:T] - center[None]
    dev = jnp.sum(both[:, T:] + n * off * off, axis=0)
    total = jnp.dot(dev, gm, precision=HI, preferred_element_type=F32)
    spread = total * (1.0 / (n * w.nd * GSIZE))
    return center, 1.0 / jnp.sqrt(spread + EPSILON)


SIDES = ((0, -1), (0, 1), (-1, 0), (1, 0), (-1, -1), (-1, 1), (1, -1), (1, 1))


def halo_pack(p, n, col_s, cor_s):
    for f in range(n):
        col_s[0, f] = p[f, 1 : 1 + H, 0, :]
        col_s[1, f] = p[f, 1 : 1 + H, W - 1, :]
        for j, (dy, dx) in enumerate(SIDES[4:]):
            row = 1 if dy < 0 else H
            lane = 0 if dx < 0 else W - 1
            cor_s[j, f : f + 1, :] = p[f, row, lane : lane + 1, :]


def halo_copies(w, p, col_s, col_r, cor_s, cor_r, ssem, rsem):
    out = []
    for j, (dy, dx) in enumerate(SIDES):
        dev = w.shift(dy, dx)
        if j < 2:
            src, dst = col_s.at[j], col_r.at[j]
        elif j < 4:
            row, land = (1, HP - 1) if dy < 0 else (H, 0)
            src, dst = p.at[:, row, 0:W, :], p.at[:, land, 0:W, :]
        else:
            src, dst = cor_s.at[j - 4], cor_r.at[j - 4]
        out.append(rcopy(src, dst, ssem.at[j], rsem.at[j], dev))
    return out


def halo_unpack(p, n, col_r, cor_r):
    for f in range(n):
        p[f, 1 : 1 + H, W, :] = col_r[0, f]
        p[f, 1 : 1 + H, PW - 1, :] = col_r[1, f]
        for j, (dy, dx) in enumerate(SIDES[4:]):
            row = HP - 1 if dy < 0 else 0
            lane = W if dx < 0 else PW - 1
            p[f, row, lane : lane + 1, :] = cor_r[j, f : f + 1, :]


def halo_scratch(n):
    return [
        pltpu.VMEM((2, n, H, C), F32),
        pltpu.VMEM((2, n, H, C), F32),
        pltpu.VMEM((4, 8, C), F32),
        pltpu.VMEM((4, 8, C), F32),
        pltpu.SemaphoreType.DMA((8,)),
        pltpu.SemaphoreType.DMA((8,)),
    ]


def gather_scratch(nd):
    return [
        pltpu.VMEM((nd, 8, C), F32),
        pltpu.SemaphoreType.DMA((nd,)),
        pltpu.SemaphoreType.DMA((nd,)),
    ]


def tile_moments(read, n):
    cells = 1.0 / (H * W)
    means, devs = [], []
    for f in range(n):

        def add(i, acc, f=f):
            return acc + read(f, i)

        total = lax.fori_loop(0, H, add, jnp.zeros((W, C), F32), unroll=4)
        mean = jnp.sum(total, axis=0, keepdims=True) * cells

        def add2(i, acc, f=f, mean=mean):
            v = read(f, i) - mean
            return acc + v * v

        total = lax.fori_loop(0, H, add2, jnp.zeros((W, C), F32), unroll=4)
        means.append(mean)
        devs.append(jnp.sum(total, axis=0, keepdims=True))
    return means, devs


def k_open(dims, lat, rg, p, st, *scratch):
    w = Where(dims)
    hal, gat = scratch[:6], scratch[6:]
    col_s, col_r, cor_s, cor_r, hs, hr = hal
    buf, gs, gr = gat

    def fill(i, _):
        for f, ref in ((0, lat), (1, rg)):
            p[f, i + 1, 0:W, :] = ref[i]
            p[f, i + 1, W:PW, :] = jnp.zeros((PW - W, C), F32)
        return 0

    lax.fori_loop(0, H, fill, 0)
    for f in range(2):
        for row in (0, HP - 1):
            p[f, row] = jnp.zeros((PW, C), F32)
    cor_s[...] = jnp.zeros_like(cor_s)
    halo_pack(p, 2, col_s, cor_s)
    greet(w.tiles())
    copies = halo_copies(w, p, col_s, col_r, cor_s, cor_r, hs, hr)
    for cp in copies:
        cp.start()
    means, devs = tile_moments(lambda f, i: lat[i], 1)
    buf[w.me] = jnp.concatenate(means * T + devs * T, axis=0)
    sent = gather_start(w, buf, gs, gr)
    gather_wait(w, buf, gs, gr, sent)
    center, inv = moments(buf, w)
    st[0:T] = center
    st[T:] = inv
    for cp in copies:
        cp.wait()
    halo_unpack(p, 2, col_r, cor_r)


def edge_mask(w, i):
    col = lax.broadcasted_iota(jnp.int32, (PW, 1), 0)
    rows = jnp.logical_and(
        jnp.logical_or(i > 0, w.y > 0), jnp.logical_or(i < HP - 1, w.y < w.ny - 1)
    )
    left = jnp.where(w.x > 0, 1, 0)
    right = jnp.where(w.x < w.nx - 1, 1, 0)
    inside = jnp.where(col == PW - 1, left, jnp.where(col == W, right, 1))
    return inside * jnp.where(rows, 1, 0) > 0


def pack_row(ab, k, i, v):
    shifts = [pltpu.roll(v, 1, 0)[0:W], v[0:W], pltpu.roll(v, PW - 1, 0)[0:W]]
    for s in range(3):
        ab[k, i, :, 256 * s : 256 * s + 256] = shifts[s][:, 0:256].astype(BF16)
    tail = jnp.concatenate(
        [u[:, 256:C] for u in shifts] + [jnp.zeros((W, 64), F32)], axis=1
    )
    ab[k, i, :, 768:AW] = tail.astype(BF16)


def window(ab, k, r):
    return ab[k, r : r + H].reshape(H * W, AW)


def conv(ab, k, wt):
    acc = jnp.dot(window(ab, k, 0), wt[0], preferred_element_type=F32)
    acc += jnp.dot(window(ab, k, 1), wt[1], preferred_element_type=F32)
    acc += jnp.dot(window(ab, k, 2), wt[2], preferred_element_type=F32)
    return acc.reshape(H, W, C)


def build_act(w, p, st, mod, ab, k, f):
    center = st[pl.ds(k, 1), :]
    inv = st[pl.ds(T + k, 1), :]
    m = mod[pl.ds(k, 1), :]

    def row(i, _):
        pre = (p[f, i] - center) * inv * m
        act = pre / (1.0 + jnp.exp(-pre))
        act = jnp.where(edge_mask(w, i), act, 0.0)
        pack_row(ab, k, i, act)
        return 0

    lax.fori_loop(0, HP, row, 0, unroll=2)


def k_first(dims, coef, p, st, mod, wr, wd, noise, run, ab, dact, abu):
    w = Where(dims)

    def step(k, _):
        cs, cd, cn = coef[0, k], coef[1, k], coef[2, k]
        build_act(w, p, st, mod, ab, k, 0)
        out = conv(ab, k, wr)
        lat = p[0, 1 : 1 + H, 0:W, :]
        inc = cs * lat + cd * (lat + out) + cn * noise[k].astype(F32)
        prev = run[jnp.maximum(k - 1, 0)]
        run[k] = jnp.where(k > 0, prev, 0.0) + inc

        def row(i, _):
            up = jnp.where(edge_mask(w, i), cd * p[1, i], 0.0)
            pack_row(abu, k, i, up)
            return 0

        lax.fori_loop(0, HP, row, 0, unroll=2)
        dact[k] = conv(abu, k, wd)
        return 0

    lax.fori_loop(0, T, step, 0)


def k_second(dims, coef, p, st, mod, wr, noise, dact, run, ab, dn, cs_out):
    w = Where(dims)

    def step(k, _):
        cs, cd, cn = coef[0, k], coef[1, k], coef[2, k]
        build_act(w, p, st, mod, ab, k, k)
        out = conv(ab, k, wr)
        v = p[k, 1 : 1 + H, 0:W, :]
        inc = cs * v + cd * (v + out) + cn * noise[k].astype(F32)
        prev = run[jnp.maximum(k - 1, 0)]
        run[k] = jnp.where(k > 0, prev, 0.0) + inc
        center = st[pl.ds(k, 1), :]
        inv = st[pl.ds(T + k, 1), :]
        m = mod[pl.ds(k, 1), :]

        def row(i, acc):
            plain, cross = acc
            norm = (p[k, i + 1, 0:W, :] - center) * inv
            pre = norm * m
            sig = 1.0 / (1.0 + jnp.exp(-pre))
            d = dact[k, i] * sig * (1.0 + pre * (1.0 - sig)) * m
            dn[k, i] = d
            return plain + d, cross + d * norm

        zero = jnp.zeros((W, C), F32)
        plain, cross = lax.fori_loop(0, H, row, (zero, zero), unroll=2)
        cs_out[pl.ds(k, 1), :] = jnp.sum(plain, axis=0, keepdims=True)
        cs_out[pl.ds(T + k, 1), :] = jnp.sum(cross, axis=0, keepdims=True)
        return 0

    lax.fori_loop(0, T, step, 0)


def k_weight(dims, coef, rg, adj, ab1, ab2, g, upt):
    for k in range(T):
        cd = coef[1, k]
        up1 = (cd * adj[k]).reshape(H * W, C).astype(BF16)
        up2 = (cd * rg[...]).reshape(H * W, C).astype(BF16)
        upt[:, pl.ds(k * H * W, H * W)] = up1.T
        upt[:, pl.ds((T + k) * H * W, H * W)] = up2.T
    nt = dims[0]
    for r in range(3):
        for j in range(AW // 256):
            rhs = [
                ab[k, r : r + H, :, 256 * j : 256 * j + 256].reshape(H * W, 256)
                for ab in (ab1, ab2)
                for k in range(T)
            ]
            out = jnp.dot(
                upt[...], jnp.concatenate(rhs, axis=0), preferred_element_type=F32
            )
            for half in range(2):
                chunk = r * 8 + j * 2 + half
                part = out[:, 128 * half : 128 * half + 128]
                g[:, 5 * chunk : 5 * chunk + 5] = part.reshape(nt, 5, 8, 128)
    g[:, 120:128] = jnp.zeros((nt, 8, 8, 128), F32)


CHUNKS = 4


def chain_scratch():
    half = (H // 2, W, C)
    return [
        pltpu.VMEM(half, F32),
        pltpu.VMEM(half, F32),
        pltpu.VMEM(half, F32),
        pltpu.VMEM(half, F32),
        pltpu.VMEM((H, W, C), F32),
        pltpu.SemaphoreType.DMA((1 + 2 * CHUNKS,)),
        pltpu.SemaphoreType.DMA((1 + 2 * CHUNKS,)),
    ]


def chain_start(w, total, scr, rev):
    prx, inc, outc, offp, off, ss, rs = scr
    hh = H // 2
    c = lax.rem(w.tm, 2)
    partner = w.line()[0]
    cp = rcopy(total.at[pl.ds(hh * (1 - c), hh)], prx, ss.at[0], rs.at[0], partner)
    cp.start()


def chain_steps(w, total, scr, rev):
    prx, inc, outc, offp, off, ss, rs = scr
    hh = H // 2
    per = hh // CHUNKS
    c = lax.rem(w.tm, 2)
    x = lax.div(w.tm, 2)
    chips = w.nt // 2
    partner, nxt, prv = w.line()
    if rev:
        nxt, prv = prv, nxt
        x = chips - 1 - x
    second = (c == 0) if rev else (c == 1)
    cp0 = rcopy(total.at[pl.ds(hh * (1 - c), hh)], prx, ss.at[0], rs.at[0], partner)
    cp0.wait_recv()

    @pl.when(x == 0)
    def _():
        inc[...] = jnp.zeros_like(inc)

    def fwd(j):
        part = pl.ds(j * per, per)
        return rcopy(outc.at[part], inc.at[part], ss.at[1 + j], rs.at[1 + j], nxt)

    def give(j):
        part = pl.ds(j * per, per)
        return rcopy(
            offp.at[part],
            off.at[pl.ds(hh * c + j * per, per)],
            ss.at[1 + CHUNKS + j],
            rs.at[1 + CHUNKS + j],
            partner,
        )

    for j in range(CHUNKS):
        part = pl.ds(j * per, per)
        own = pl.ds(hh * c + j * per, per)

        @pl.when(x > 0)
        def _():
            fwd(j).wait_recv()

        got = inc[part]
        mine = total[own]
        other = prx[part]

        @pl.when(x < chips - 1)
        def _():
            outc[part] = got + (mine + other)
            fwd(j).start()

        off[own] = got + jnp.where(second, other, 0.0)
        offp[part] = got + jnp.where(second, 0.0, mine)
        give(j).start()
        yield
    cp0.wait_send()
    for j in range(CHUNKS):
        give(j).wait_send()
        rcopy(
            offp.at[pl.ds(j * per, per)],
            off.at[pl.ds(hh * (1 - c) + j * per, per)],
            ss.at[1 + CHUNKS + j],
            rs.at[1 + CHUNKS + j],
            partner,
        ).wait_recv()

        @pl.when(x < chips - 1)
        def _():
            fwd(j).wait_send()


def k_states(dims, lat, run, sp, st, *scratch):
    w = Where(dims)
    hal, gat, ch = scratch[:6], scratch[6:9], scratch[9:16]
    col_s, col_r, cor_s, cor_r, hs, hr = hal
    buf, gs, gr = gat
    off = ch[4]
    cor_s[...] = jnp.zeros_like(cor_s)

    def clear(i, _):
        for k in range(T):
            sp[k, i] = jnp.zeros((PW, C), F32)
        return 0

    lax.fori_loop(0, HP, clear, 0)
    greet(w.tiles() + w.line())
    total = run.at[T - 1]
    chain_start(w, total, ch, False)
    for _ in chain_steps(w, total, ch, False):
        pass

    def fill(i, _):
        base = lat[i]
        o = off[i]
        sp[0, i + 1, 0:W, :] = base + o
        for k in range(1, T):
            sp[k, i + 1, 0:W, :] = base + (o + run[k - 1, i])
        return 0

    lax.fori_loop(0, H, fill, 0, unroll=2)
    halo_pack(sp, T, col_s, cor_s)
    copies = halo_copies(w, sp, col_s, col_r, cor_s, cor_r, hs, hr)
    for cp in copies:
        cp.start()
    means, devs = tile_moments(lambda f, i: sp[f, i + 1, 0:W, :], T)
    buf[w.me] = jnp.concatenate(means + devs, axis=0)
    sent = gather_start(w, buf, gs, gr)
    gather_wait(w, buf, gs, gr, sent)
    center, inv = moments(buf, w)
    st[0:T] = center
    st[T:] = inv
    for cp in copies:
        cp.wait()
    halo_unpack(sp, T, col_r, cor_r)


def k_adjoint(dims, coef, lat, rg, sp, st, dn, cs_in, run, traj, adj, suf, *scratch):
    w = Where(dims)
    gat, c1, c2 = scratch[:3], scratch[3:10], scratch[10:17]
    buf, gs, gr = gat
    buf[w.me] = cs_in[...]
    greet(w.tiles() + w.line())
    sent = gather_start(w, buf, gs, gr)
    chain_start(w, run.at[T - 1], c2, False)
    gather_wait(w, buf, gs, gr, sent)
    sums = jnp.sum(buf[...], axis=0)
    means = jnp.dot(sums, group_matrix(), precision=HI, preferred_element_type=F32)
    means = means * (1.0 / (H * W * w.nd * GSIZE))

    def row(i, _):
        rgv = rg[i]
        acc = None
        for k in range(T - 1, -1, -1):
            center, inv = st[k : k + 1, :], st[T + k : T + k + 1, :]
            plain, cross = means[k : k + 1, :], means[T + k : T + k + 1, :]
            norm = (sp[k, i + 1, 0:W, :] - center) * inv
            d = (dn[k, i] - plain - norm * cross) * inv
            t = coef[0, k] * rgv + (coef[1, k] * rgv + d)
            acc = t if acc is None else acc + t
            suf[k, i] = acc
        return 0

    lax.fori_loop(0, H, row, 0)
    total = suf.at[0]
    chain_start(w, total, c1, True)
    for _ in itertools.chain(
        chain_steps(w, total, c1, True), chain_steps(w, run.at[T - 1], c2, False)
    ):
        pass
    off1, off2 = c1[4], c2[4]

    def fin(i, _):
        o1, o2, base = off1[i], off2[i], lat[i]
        for k in range(T):
            adj[k, i] = o1 + suf[k + 1, i] if k + 1 < T else o1
            traj[k, i] = base + (o2 + run[k, i])
        return 0

    lax.fori_loop(0, H, fin, 0)


def k_reduce(dims, g, out, ra, s, ry, rz, s1, rz1, ry1, s2, rx, *sems):
    w = Where(dims)
    chips = w.nt // 2
    c = lax.rem(w.tm, 2)
    xme = lax.div(w.tm, 2)
    ny, nx = w.ny, w.nx
    sa, sb, sc_, sd, se = sems[0::2]
    qa, qb, qc, qd, qe = sems[1::2]
    partner = w.line()[0]

    def chip(d):
        q = lax.rem(xme + d, chips)
        return q, w.dev(2 * q + c, w.y, w.x)

    greet(w.tiles() + [partner] + [chip(d)[1] for d in range(1, chips)])
    done = []

    def go(cp):
        cp.start()
        done.append(cp)

    go(rcopy(g.at[:, 1 - c], ra, sa.at[0], qa.at[0], partner))
    done[-1].wait_recv()
    for x in range(chips):

        def add(i, _, x=x):
            for j in range(nx):
                s[x, i, j] = g[x, c, i, j] + ra[x, i, j]
            return 0

        lax.fori_loop(0, ny, add, 0)
    for d in range(1, nx):
        q = lax.rem(w.x + d, nx)
        go(rcopy(s.at[:, :, q, 0:4], rz.at[w.x], sb.at[d], qb.at[w.x], w.shift(0, d)))
    for d in range(1, ny):
        q = lax.rem(w.y + d, ny)
        go(rcopy(s.at[:, q, :, 4:8], ry.at[w.y], sb.at[nx + d], qb.at[nx + w.y], w.shift(d, 0)))
    for d in range(1, nx):
        q = lax.rem(w.x + d, nx)
        rcopy(rz.at[q], rz.at[q], sb.at[d], qb.at[q], partner).wait_recv()
    for d in range(1, ny):
        q = lax.rem(w.y + d, ny)
        rcopy(ry.at[q], ry.at[q], sb.at[nx + d], qb.at[nx + q], partner).wait_recv()
    for x in range(chips):
        for i in range(ny):
            acc = s[x, i, w.x, 0:4]
            for d in range(1, nx):
                acc += rz[lax.rem(w.x + d, nx), x, i]
            s1[0, x, i] = acc
        for j in range(nx):
            acc = s[x, w.y, j, 4:8]
            for d in range(1, ny):
                acc += ry[lax.rem(w.y + d, ny), x, j]
            s1[1, x, j] = acc
    for d in range(1, ny):
        q = lax.rem(w.y + d, ny)
        go(rcopy(s1.at[0, :, q], rz1.at[w.y], sc_.at[d], qc.at[w.y], w.shift(d, 0)))
    for d in range(1, nx):
        q = lax.rem(w.x + d, nx)
        go(rcopy(s1.at[1, :, q], ry1.at[w.x], sc_.at[ny + d], qc.at[ny + w.x], w.shift(0, d)))
    for d in range(1, ny):
        q = lax.rem(w.y + d, ny)
        rcopy(rz1.at[q], rz1.at[q], sc_.at[d], qc.at[q], partner).wait_recv()
    for d in range(1, nx):
        q = lax.rem(w.x + d, nx)
        rcopy(ry1.at[q], ry1.at[q], sc_.at[ny + d], qc.at[ny + q], partner).wait_recv()
    for x in range(chips):
        acc = s1[0, x, w.y]
        for d in range(1, ny):
            acc += rz1[lax.rem(w.y + d, ny), x]
        s2[x, 0:4] = acc
        acc = s1[1, x, w.x]
        for d in range(1, nx):
            acc += ry1[lax.rem(w.x + d, nx), x]
        s2[x, 4:8] = acc
    for d in range(1, chips):
        q, dev = chip(d)
        go(rcopy(s2.at[q], rx.at[xme], sd.at[d], qd.at[xme], dev))
    for d in range(1, chips):
        q, dev = chip(d)
        rcopy(rx.at[q], rx.at[q], sd.at[d], qd.at[q], dev).wait_recv()
    acc = s2[xme]
    for d in range(1, chips):
        acc += rx[lax.rem(xme + d, chips)]
    out[w.me] = acc
    sent = gather_start(w, out, se, qe)
    gather_wait(w, out, se, qe, sent)
    for cp in done:
        cp.wait_send()


def call(kernel, dims, args, outs, scratch, cid=None, smem=0):
    params = dict(vmem_limit_bytes=VLIM)
    if cid is not None:
        params.update(collective_id=cid, has_side_effects=True)
    return pl.pallas_call(
        functools.partial(kernel, dims),
        out_shape=tuple(jax.ShapeDtypeStruct(s, d) for s, d in outs),
        in_specs=[SM] * smem + [VM] * (len(args) - smem),
        out_specs=tuple(VM for _ in outs),
        scratch_shapes=scratch,
        compiler_params=pltpu.CompilerParams(**params),
        name=kernel.__name__,
    )(*args)


def pack_weight(wt):
    main = wt[:, :, 0:256].reshape(3, 768, C)
    tail = wt[:, :, 256:C].reshape(3, 192, C)
    return jnp.concatenate([main, tail, jnp.zeros((3, 64, C), wt.dtype)], axis=1)


def shards(dims, latent, noise, coef_state, coef_drift, coef_noise, step_index, table, gain, weight, rg):
    nt, ny, nx = dims
    nd = ny * nx
    ids = jnp.arange(table.shape[0], dtype=jnp.int32)
    hot = (step_index[:, None] == ids[None, :]).astype(F32)
    mod = gain[None, :] * (1.0 + jnp.dot(hot, table, precision=HI))
    coef = jnp.stack([coef_state, coef_drift, coef_noise])
    wr = pack_weight(weight)
    wd = pack_weight(jnp.transpose(weight[::-1, ::-1], (0, 1, 3, 2)))
    field = (T, H, W, C)
    abs_ = (T, HP, W, AW)
    p, st = call(
        k_open, dims, (latent, rg), [((2, HP, PW, C), F32), ((8, C), F32)],
        halo_scratch(2) + gather_scratch(nd), cid=0,
    )
    run, ab1, dact = call(
        k_first, dims, (coef, p, st, mod, wr, wd, noise),
        [(field, F32), (abs_, BF16), (field, F32)], [pltpu.VMEM(abs_, BF16)], smem=1,
    )
    sp, st2 = call(
        k_states, dims, (latent, run), [((T, HP, PW, C), F32), ((8, C), F32)],
        halo_scratch(T) + gather_scratch(nd) + chain_scratch(), cid=1,
    )
    run2, ab2, dn, cs = call(
        k_second, dims, (coef, sp, st2, mod, wr, noise, dact),
        [(field, F32), (abs_, BF16), (field, F32), ((8, C), F32)], [], smem=1,
    )
    traj, adj = call(
        k_adjoint, dims, (coef, latent, rg, sp, st2, dn, cs, run2),
        [(field, F32), (field, F32)],
        [pltpu.VMEM(field, F32)] + gather_scratch(nd) + chain_scratch() + chain_scratch(),
        cid=2, smem=1,
    )
    (g,) = call(
        k_weight, dims, (coef, rg, adj, ab1, ab2), [((nt, 128, 8, 128), F32)],
        [pltpu.VMEM((C, 2 * T * H * W), BF16)], smem=1,
    )
    chips = nt // 2
    per = 128 // nd
    dma = pltpu.SemaphoreType.DMA
    (out,) = call(
        k_reduce, dims, (g.reshape(chips, 2, ny, nx, per, 8, 128),), [((nd, per, 8, 128), F32)],
        [
            pltpu.VMEM((chips, ny, nx, per, 8, 128), F32),
            pltpu.VMEM((chips, ny, nx, per, 8, 128), F32),
            pltpu.VMEM((ny, chips, nx, per // 2, 8, 128), F32),
            pltpu.VMEM((nx, chips, ny, per // 2, 8, 128), F32),
            pltpu.VMEM((2, chips, 4, per // 2, 8, 128), F32),
            pltpu.VMEM((ny, chips, per // 2, 8, 128), F32),
            pltpu.VMEM((nx, chips, per // 2, 8, 128), F32),
            pltpu.VMEM((chips, per, 8, 128), F32),
            pltpu.VMEM((chips, per, 8, 128), F32),
            dma((1,)), dma((1,)),
            dma((nx + ny,)), dma((nx + ny,)),
            dma((nx + ny,)), dma((nx + ny,)),
            dma((chips,)), dma((chips,)),
            dma((nd,)), dma((nd,)),
        ],
        cid=3,
    )
    tiles = out.reshape(128, 8, 128)[:120].reshape(3, 8, 40, 128)
    flat = jnp.transpose(tiles, (0, 2, 1, 3)).reshape(3, 40, AW)
    main = flat[:, :, 0:768].reshape(3, 40, 3, 256)
    tail = flat[:, :, 768:960].reshape(3, 40, 3, 64)
    grad = jnp.transpose(jnp.concatenate([main, tail], axis=3), (0, 2, 3, 1))
    return traj, grad


def solution(mesh):
    dims = (mesh.shape["tm"], mesh.shape["sy"], mesh.shape["sx"])
    tile = P("sy", "sx", None)
    full = P("tm", "sy", "sx", None)
    step = P("tm")
    return jax.shard_map(
        functools.partial(shards, dims),
        mesh=mesh,
        in_specs=(tile, full, step, step, step, step, P(), P(), P(), tile),
        out_specs=(full, P(None, None, None, "tm")),
        check_vma=False,
    )
```

```python
import functools

import jax
import jax.numpy as jnp
from jax import lax
from jax.experimental import pallas as pl
from jax.experimental.pallas import tpu as pltpu
from jax.sharding import PartitionSpec as P

MESH = pl.DeviceIdType.MESH
VM = pl.BlockSpec(memory_space=pltpu.VMEM)
SM = pl.BlockSpec(memory_space=pltpu.SMEM)
F32 = jnp.float32
BF16 = jnp.bfloat16
HI = lax.Precision.HIGHEST
EPSILON = 1e-05
GSIZE = 10
T = 4
H = 16
W = 24
C = 320
PW = 32
HP = H + 2
AW = 1024
VLIM = 60 << 20


def rcopy(src, dst, ssem, rsem, dev):
    return pltpu.make_async_remote_copy(
        src_ref=src, dst_ref=dst, send_sem=ssem, recv_sem=rsem, device_id=dev, device_id_type=MESH
    )


def greet(devs):
    sem = pltpu.get_barrier_semaphore()
    for dev in devs:
        pl.semaphore_signal(sem, inc=1, device_id=dev, device_id_type=MESH)


class Where:
    def __init__(self, dims):
        self.nt, self.ny, self.nx = dims
        self.tm = lax.axis_index("tm")
        self.y = lax.axis_index("sy")
        self.x = lax.axis_index("sx")
        self.nd = self.ny * self.nx
        self.me = self.y * self.nx + self.x

    def dev(self, tm, y, x):
        return (tm, y, x)

    def tile(self, d):
        q = lax.rem(self.me + d, self.nd)
        return q, self.dev(self.tm, lax.div(q, self.nx), lax.rem(q, self.nx))

    def shift(self, dy, dx):
        return self.dev(
            self.tm,
            lax.rem(self.y + dy + self.ny, self.ny),
            lax.rem(self.x + dx + self.nx, self.nx),
        )

    def tiles(self):
        return [self.tile(d)[1] for d in range(1, self.nd)]

    def line(self):
        c = lax.rem(self.tm, 2)
        return [
            self.dev(self.tm + 1 - 2 * c, self.y, self.x),
            self.dev(lax.rem(self.tm + 2, self.nt), self.y, self.x),
            self.dev(lax.rem(self.tm + self.nt - 2, self.nt), self.y, self.x),
        ]


def gather_start(w, buf, ssem, rsem):
    out = []
    for d in range(1, w.nd):
        _, dev = w.tile(d)
        cp = rcopy(buf.at[w.me], buf.at[w.me], ssem.at[d], rsem.at[w.me], dev)
        cp.start()
        out.append(cp)
    return out


def gather_wait(w, buf, ssem, rsem, sent):
    for cp in sent:
        cp.wait_send()
    for d in range(1, w.nd):
        q, dev = w.tile(d)
        rcopy(buf.at[q], buf.at[q], ssem.at[d], rsem.at[q], dev).wait_recv()


def group_matrix():
    row = lax.broadcasted_iota(jnp.int32, (C, C), 0)
    col = lax.broadcasted_iota(jnp.int32, (C, C), 1)
    same = ((row * 6554) >> 16) == ((col * 6554) >> 16)
    return same.astype(F32)


def moments(buf, w):
    gm = group_matrix()
    n = float(H * W)
    both = buf[...]
    mean = jnp.sum(both[:, 0:T], axis=0) * (1.0 / w.nd)
    center = jnp.dot(mean, gm, precision=HI, preferred_element_type=F32) * (1.0 / GSIZE)
    off = both[:, 0:T] - center[None]
    dev = jnp.sum(both[:, T:] + n * off * off, axis=0)
    total = jnp.dot(dev, gm, precision=HI, preferred_element_type=F32)
    spread = total * (1.0 / (n * w.nd * GSIZE))
    return center, 1.0 / jnp.sqrt(spread + EPSILON)


SIDES = ((0, -1), (0, 1), (-1, 0), (1, 0), (-1, -1), (-1, 1), (1, -1), (1, 1))


def halo_pack(p, n, col_s, cor_s):
    for f in range(n):
        col_s[0, f] = p[f, 1 : 1 + H, 0, :]
        col_s[1, f] = p[f, 1 : 1 + H, W - 1, :]
        for j, (dy, dx) in enumerate(SIDES[4:]):
            row = 1 if dy < 0 else H
            lane = 0 if dx < 0 else W - 1
            cor_s[j, f : f + 1, :] = p[f, row, lane : lane + 1, :]


def halo_copies(w, p, col_s, col_r, cor_s, cor_r, ssem, rsem):
    out = []
    for j, (dy, dx) in enumerate(SIDES):
        dev = w.shift(dy, dx)
        if j < 2:
            src, dst = col_s.at[j], col_r.at[j]
        elif j < 4:
            row, land = (1, HP - 1) if dy < 0 else (H, 0)
            src, dst = p.at[:, row, 0:W, :], p.at[:, land, 0:W, :]
        else:
            src, dst = cor_s.at[j - 4], cor_r.at[j - 4]
        out.append(rcopy(src, dst, ssem.at[j], rsem.at[j], dev))
    return out


def halo_unpack(p, n, col_r, cor_r):
    for f in range(n):
        p[f, 1 : 1 + H, W, :] = col_r[0, f]
        p[f, 1 : 1 + H, PW - 1, :] = col_r[1, f]
        for j, (dy, dx) in enumerate(SIDES[4:]):
            row = HP - 1 if dy < 0 else 0
            lane = W if dx < 0 else PW - 1
            p[f, row, lane : lane + 1, :] = cor_r[j, f : f + 1, :]


def halo_scratch(n):
    return [
        pltpu.VMEM((2, n, H, C), F32),
        pltpu.VMEM((2, n, H, C), F32),
        pltpu.VMEM((4, 8, C), F32),
        pltpu.VMEM((4, 8, C), F32),
        pltpu.SemaphoreType.DMA((8,)),
        pltpu.SemaphoreType.DMA((8,)),
    ]


def gather_scratch(nd):
    return [
        pltpu.VMEM((nd, 8, C), F32),
        pltpu.SemaphoreType.DMA((nd,)),
        pltpu.SemaphoreType.DMA((nd,)),
    ]


def tile_moments(read, n):
    cells = 1.0 / (H * W)
    means, devs = [], []
    for f in range(n):

        def add(i, acc, f=f):
            return acc + read(f, i)

        total = lax.fori_loop(0, H, add, jnp.zeros((W, C), F32), unroll=4)
        mean = jnp.sum(total, axis=0, keepdims=True) * cells

        def add2(i, acc, f=f, mean=mean):
            v = read(f, i) - mean
            return acc + v * v

        total = lax.fori_loop(0, H, add2, jnp.zeros((W, C), F32), unroll=4)
        means.append(mean)
        devs.append(jnp.sum(total, axis=0, keepdims=True))
    return means, devs


CH = 4
ROWS = H // CH


def edge_mask(w, i):
    col = lax.broadcasted_iota(jnp.int32, (PW, 1), 0)
    rows = jnp.logical_and(
        jnp.logical_or(i > 0, w.y > 0), jnp.logical_or(i < HP - 1, w.y < w.ny - 1)
    )
    left = jnp.where(w.x > 0, 1, 0)
    right = jnp.where(w.x < w.nx - 1, 1, 0)
    inside = jnp.where(col == PW - 1, left, jnp.where(col == W, right, 1))
    return inside * jnp.where(rows, 1, 0) > 0


def pack_row(ab, k, i, v):
    shifts = [pltpu.roll(v, 1, 0)[0:W], v[0:W], pltpu.roll(v, PW - 1, 0)[0:W]]
    for s in range(3):
        ab[k, i, :, 256 * s : 256 * s + 256] = shifts[s][:, 0:256].astype(BF16)
    tail = jnp.concatenate(
        [u[:, 256:C] for u in shifts] + [jnp.zeros((W, 64), F32)], axis=1
    )
    ab[k, i, :, 768:AW] = tail.astype(BF16)


def conv_rows(ab, j, wt):
    acc = None
    for r in range(3):
        lhs = ab[:, pl.ds(ROWS * j + r, ROWS)].reshape(T * ROWS * W, AW)
        out = jnp.dot(lhs, wt[r], preferred_element_type=F32)
        acc = out if acc is None else acc + out
    return acc.reshape(T, ROWS, W, C)


def pack_weights(weight, wr, wd):
    for r in range(3):
        for dst in (wr, wd):
            dst[r, 960:AW] = jnp.zeros((64, C), BF16)
        for s in range(3):
            one = weight[r, s]
            wr[r, 256 * s : 256 * s + 256] = one[0:256]
            wr[r, 768 + 64 * s : 832 + 64 * s] = one[256:C]
            turned = weight[2 - r, 2 - s].T
            wd[r, 256 * s : 256 * s + 256] = turned[0:256]
            wd[r, 768 + 64 * s : 832 + 64 * s] = turned[256:C]


def build_act(w, p, field, st, mod, ab, k):
    center = st[pl.ds(k, 1), :]
    inv = st[pl.ds(T + k, 1), :]
    m = mod[pl.ds(k, 1), :]

    def row(i, _):
        pre = (p[field, i] - center) * inv * m
        act = pre / (1.0 + jnp.exp(-pre))
        act = jnp.where(edge_mask(w, i), act, 0.0)
        pack_row(ab, k, i, act)
        return 0

    lax.fori_loop(0, HP, row, 0, unroll=2)


def chain_scratch():
    part = (CH, ROWS // 2, W, C)
    return [
        pltpu.VMEM(part, F32),
        pltpu.VMEM(part, F32),
        pltpu.VMEM(part, F32),
        pltpu.VMEM(part, F32),
        pltpu.VMEM((H, W, C), F32),
        pltpu.SemaphoreType.DMA((3 * CH,)),
        pltpu.SemaphoreType.DMA((3 * CH,)),
    ]


class Chain:
    def __init__(self, w, total, scr, rev):
        self.w, self.total, self.scr = w, total, scr
        self.prx, self.inc, self.outc, self.offp, self.off, self.ss, self.rs = scr
        self.c = lax.rem(w.tm, 2)
        self.chips = w.nt // 2
        x = lax.div(w.tm, 2)
        self.partner, nxt, prv = w.line()
        self.nxt = prv if rev else nxt
        self.x = self.chips - 1 - x if rev else x
        self.second = (self.c == 0) if rev else (self.c == 1)

    def rows(self, j, c):
        hh = ROWS // 2
        return pl.ds(ROWS * j + hh * c, hh)

    def pair(self, j):
        return rcopy(
            self.total.at[self.rows(j, 1 - self.c)], self.prx.at[j], self.ss.at[j], self.rs.at[j], self.partner
        )

    def fwd(self, j):
        return rcopy(
            self.outc.at[j], self.inc.at[j], self.ss.at[CH + j], self.rs.at[CH + j], self.nxt
        )

    def give(self, j, c):
        return rcopy(
            self.offp.at[j], self.off.at[self.rows(j, c)],
            self.ss.at[2 * CH + j], self.rs.at[2 * CH + j], self.partner,
        )

    def step(self, j):
        self.pair(j).wait_recv()

        @pl.when(self.x == 0)
        def _():
            self.inc[j] = jnp.zeros((ROWS // 2, W, C), F32)

        @pl.when(self.x > 0)
        def _():
            self.fwd(j).wait_recv()

        mine = self.total[self.rows(j, self.c)]

        @pl.when(self.x < self.chips - 1)
        def _():
            self.outc[j] = self.inc[j] + (mine + self.prx[j])
            self.fwd(j).start()

        got = self.inc[j]
        self.off[self.rows(j, self.c)] = got + jnp.where(self.second, self.prx[j], 0.0)
        self.offp[j] = got + jnp.where(self.second, 0.0, mine)
        self.give(j, self.c).start()

    def steps(self):
        for j in range(CH):
            self.step(j)

    def finish(self):
        for j in range(CH):
            self.pair(j).wait_send()
            self.give(j, self.c).wait_send()
            self.give(j, 1 - self.c).wait_recv()

            @pl.when(self.x < self.chips - 1)
            def _(j=j):
                self.fwd(j).wait_send()


def wgrad(upt, ab, g, r, first):
    chips = g.shape[0]
    for j in range(AW // 256):
        rhs = [
            ab[k, pl.ds(r, H), :, 256 * j : 256 * j + 256].reshape(H * W, 256) for k in range(T)
        ]
        out = jnp.dot(upt[...], jnp.concatenate(rhs, axis=0), preferred_element_type=F32)
        for half in range(2):
            place = pl.ds(5 * (r * 8 + j * 2 + half), 5)
            part = out[:, 128 * half : 128 * half + 128].reshape(chips, 2, 5, 8, 128)
            g[:, :, place] = part if first else g[:, :, place] + part


def loop_where(count, cond, step):
    def one(j, _):
        @pl.when(cond(j))
        def _():
            step(j, 0)

        return 0

    lax.fori_loop(0, count, one, 0)


def k_all(dims, *refs):
    (index, cstate, cdrift, cnoise, lat, rg, noise, weight, table, gain) = refs[:10]
    traj, out = refs[10:12]
    (p, sp, run, run2, dact, ab1, ab2, abu, wr, wd, mod, st, st2, upt1, upt2) = refs[12:27]
    hal1, hal2 = refs[27:33], refs[33:39]
    gat1, gat2, gat3 = refs[39:42], refs[42:45], refs[45:48]
    ch1, ch2, ch3 = refs[48:55], refs[55:62], refs[62:69]
    g, ra, s, ry, rz, s1, rz1, ry1, s2, rx = refs[69:79]
    sems = refs[79:]
    sa, sb, sc_, sd, se = sems[0::2]
    qa, qb, qc, qd, qe = sems[1::2]
    w = Where(dims)
    chips = w.nt // 2
    c = lax.rem(w.tm, 2)
    xme = lax.div(w.tm, 2)
    ny, nx = w.ny, w.nx
    partner = w.line()[0]

    def chip(d):
        q = lax.rem(xme + d, chips)
        return q, w.dev(2 * q + c, w.y, w.x)

    devs = w.tiles() + [partner] + [chip(d)[1] for d in range(1, chips)]
    greet(devs)

    def fill(i, _):
        for f, ref in ((0, lat), (1, rg)):
            p[f, i + 1, 0:W, :] = ref[i]
        return 0

    lax.fori_loop(0, H, fill, 0)
    for hal in (hal1, hal2):
        hal[2][...] = jnp.zeros_like(hal[2])
    halo_pack(p, 2, hal1[0], hal1[2])
    means, vars_ = tile_moments(lambda f, i: lat[i], 1)
    gat1[0][w.me] = jnp.concatenate(means * T + vars_ * T, axis=0)
    pl.semaphore_wait(pltpu.get_barrier_semaphore(), len(devs))
    sent1 = gather_start(w, *gat1)
    copies1 = halo_copies(w, p, *hal1)
    for cp in copies1:
        cp.start()

    pack_weights(weight, wr, wd)
    for k in range(T):
        mod[k : k + 1, :] = gain[...] * (1.0 + table[pl.ds(index[k], 1), :])
    turned = rg[...].reshape(H * W, C).T
    for k in range(T):
        upt2[:, k * H * W : (k + 1) * H * W] = (cdrift[k] * turned).astype(BF16)
    g[:, :, 120:128] = jnp.zeros((chips, 2, 8, 8, 128), F32)
    for cp in copies1:
        cp.wait()
    halo_unpack(p, 2, hal1[1], hal1[3])

    def up_row(i, _):
        mask = edge_mask(w, i)
        v = jnp.where(mask, p[1, i], 0.0)
        for k in range(T):
            pack_row(abu, k, i, cdrift[k] * v)
        return 0

    lax.fori_loop(0, HP, up_row, 0)
    gather_wait(w, *gat1, sent1)
    center, inv = moments(gat1[0], w)
    st[0:T] = center
    st[T:] = inv

    def act1(k, _):
        build_act(w, p, 0, st, mod, ab1, k)
        return 0

    lax.fori_loop(0, T, act1, 0)
    chain1 = Chain(w, run.at[T - 1], ch1, False)
    chain3 = Chain(w, run2.at[T - 1], ch3, False)

    def sweep(field, ab, dst, j):
        conv = conv_rows(ab, j, wr)
        rows = pl.ds(ROWS * j, ROWS)
        acc = None
        for k in range(T):
            v = field(k, j)
            inc = cstate[k] * v + cdrift[k] * (v + conv[k])
            inc = inc + cnoise[k] * noise[k, rows].astype(F32)
            acc = inc if acc is None else acc + inc
            dst[k, rows] = acc

    for j in range(CH):
        sweep(lambda k, j: lat[pl.ds(ROWS * j, ROWS)], ab1, run, j)
        chain1.pair(j).start()

    def back(j, _):
        dact[:, pl.ds(ROWS * j, ROWS)] = conv_rows(abu, j, wd)
        return 0

    early = jnp.clip(2 * (xme - 1), 0, CH)
    loop_where(CH, lambda j: j < early, back)
    chain1.steps()
    chain1.finish()

    def states(i, _):
        base = lat[i]
        o = chain1.off[i]
        sp[0, i + 1, 0:W, :] = base + o
        for k in range(1, T):
            sp[k, i + 1, 0:W, :] = base + (o + run[k - 1, i])
        return 0

    lax.fori_loop(0, H, states, 0, unroll=2)
    halo_pack(sp, T, hal2[0], hal2[2])
    copies2 = halo_copies(w, sp, *hal2)
    for cp in copies2:
        cp.start()
    means, vars_ = tile_moments(lambda f, i: sp[f, i + 1, 0:W, :], T)
    gat2[0][w.me] = jnp.concatenate(means + vars_, axis=0)
    sent2 = gather_start(w, *gat2)
    loop_where(CH, lambda j: j >= early, back)
    gather_wait(w, *gat2, sent2)
    center, inv = moments(gat2[0], w)
    st2[0:T] = center
    st2[T:] = inv

    sums = []
    for k in range(T):
        center, inv, m = st2[k : k + 1, :], st2[T + k : T + k + 1, :], mod[k : k + 1, :]

        def dnorm(i, acc, k=k, center=center, inv=inv, m=m):
            plain, cross = acc
            norm = (sp[k, i + 1, 0:W, :] - center) * inv
            pre = norm * m
            sig = 1.0 / (1.0 + jnp.exp(-pre))
            d = dact[k, i] * sig * (1.0 + pre * (1.0 - sig)) * m
            dact[k, i] = d
            return plain + d, cross + d * norm

        zero = jnp.zeros((W, C), F32)
        plain, cross = lax.fori_loop(0, H, dnorm, (zero, zero), unroll=2)
        sums.append((jnp.sum(plain, axis=0, keepdims=True), jnp.sum(cross, axis=0, keepdims=True)))
    gat3[0][w.me] = jnp.concatenate([a for a, _ in sums] + [b for _, b in sums], axis=0)
    sent3 = gather_start(w, *gat3)
    for cp in copies2:
        cp.wait()
    halo_unpack(sp, T, hal2[1], hal2[3])

    def act2(k, _):
        build_act(w, sp, k, st2, mod, ab2, k)
        return 0

    lax.fori_loop(0, T, act2, 0)
    gather_wait(w, *gat3, sent3)
    sums = jnp.sum(gat3[0][...], axis=0)
    means = jnp.dot(sums, group_matrix(), precision=HI, preferred_element_type=F32)
    means = means * (1.0 / (H * W * w.nd * GSIZE))

    chain2 = Chain(w, run.at[0], ch2, True)

    def through(i, _):
        rgv = rg[i]
        acc = None
        for k in range(T - 1, -1, -1):
            center, inv = st2[k : k + 1, :], st2[T + k : T + k + 1, :]
            plain, cross = means[k : k + 1, :], means[T + k : T + k + 1, :]
            norm = (sp[k, i + 1, 0:W, :] - center) * inv
            d = (dact[k, i] - plain - norm * cross) * inv
            t = cstate[k] * rgv + (cdrift[k] * rgv + d)
            acc = t if acc is None else acc + t
            run[k, i] = acc
        return 0

    for j in range(CH):
        lax.fori_loop(0, ROWS, lambda i, z, j=j: through(ROWS * j + i, z), 0)
        chain2.pair(j).start()

    def second(j, _):
        sweep(lambda k, j: sp[k, pl.ds(1 + ROWS * j, ROWS), 0:W, :], ab2, run2, j)
        return 0

    def weight2(r, _):
        wgrad(upt2, ab2, g, r, True)
        return 0

    n = jnp.clip(2 * chain2.x, 0, CH)
    m = jnp.where(chain2.x == chips - 1, 3, 0)
    loop_where(CH, lambda j: j < n, second)
    loop_where(3, lambda r: r < m, weight2)
    chain2.steps()
    loop_where(CH, lambda j: j >= n, second)
    for j in range(CH):
        chain3.pair(j).start()
    loop_where(3, lambda r: r >= m, weight2)
    chain2.finish()

    for k in range(T):
        adj = chain2.off[...] + run[k + 1] if k + 1 < T else chain2.off[...]
        up = (cdrift[k] * adj).reshape(H * W, C).astype(BF16)
        upt1[:, k * H * W : (k + 1) * H * W] = up.T

    def pairs(r):
        place = pl.ds(40 * r, 40)
        return rcopy(g.at[:, 1 - c, place], ra.at[:, place], sa.at[r], qa.at[r], partner)

    for r in range(3):
        wgrad(upt1, ab1, g, r, False)
        pairs(r).start()
    done = []

    def go(cp):
        cp.start()
        done.append(cp)

    per = g.shape[2] // w.nd

    def add(q, _):
        place = pl.ds(per * q, per)
        for x in range(chips):
            s[x, lax.div(q, nx), lax.rem(q, nx)] = g[x, c, place] + ra[x, place]
        return 0

    for r in range(3):
        pairs(r).wait_recv()
        lax.fori_loop(5 * r, 5 * r + 5, add, 0)
    for x in range(chips):
        s[x, ny - 1, nx - 1] = jnp.zeros((per, 8, 128), F32)
    for d in range(1, nx):
        q = lax.rem(w.x + d, nx)
        go(rcopy(s.at[:, :, q, 0:4], rz.at[w.x], sb.at[d], qb.at[w.x], w.shift(0, d)))
    for d in range(1, ny):
        q = lax.rem(w.y + d, ny)
        go(rcopy(s.at[:, q, :, 4:8], ry.at[w.y], sb.at[nx + d], qb.at[nx + w.y], w.shift(d, 0)))
    chain3.steps()
    for d in range(1, nx):
        q = lax.rem(w.x + d, nx)
        rcopy(rz.at[q], rz.at[q], sb.at[d], qb.at[q], partner).wait_recv()
    for d in range(1, ny):
        q = lax.rem(w.y + d, ny)
        rcopy(ry.at[q], ry.at[q], sb.at[nx + d], qb.at[nx + q], partner).wait_recv()

    def join(x, _):
        for i in range(ny):
            acc = s[x, i, w.x, 0:4]
            for d in range(1, nx):
                acc += rz[lax.rem(w.x + d, nx), x, i]
            s1[0, x, i] = acc
        for j in range(nx):
            acc = s[x, w.y, j, 4:8]
            for d in range(1, ny):
                acc += ry[lax.rem(w.y + d, ny), x, j]
            s1[1, x, j] = acc
        return 0

    lax.fori_loop(0, chips, join, 0)
    for d in range(1, ny):
        q = lax.rem(w.y + d, ny)
        go(rcopy(s1.at[0, :, q], rz1.at[w.y], sc_.at[d], qc.at[w.y], w.shift(d, 0)))
    for d in range(1, nx):
        q = lax.rem(w.x + d, nx)
        go(rcopy(s1.at[1, :, q], ry1.at[w.x], sc_.at[ny + d], qc.at[ny + w.x], w.shift(0, d)))
    chain3.finish()

    def final(i, _):
        o2, base = chain3.off[i], lat[i]
        for k in range(T):
            traj[k, i] = base + (o2 + run2[k, i])
        return 0

    lax.fori_loop(0, H, final, 0)
    for d in range(1, ny):
        q = lax.rem(w.y + d, ny)
        rcopy(rz1.at[q], rz1.at[q], sc_.at[d], qc.at[q], partner).wait_recv()
    for d in range(1, nx):
        q = lax.rem(w.x + d, nx)
        rcopy(ry1.at[q], ry1.at[q], sc_.at[ny + d], qc.at[ny + q], partner).wait_recv()
    for x in range(chips):
        acc = s1[0, x, w.y]
        for d in range(1, ny):
            acc += rz1[lax.rem(w.y + d, ny), x]
        s2[x, 0:4] = acc
        acc = s1[1, x, w.x]
        for d in range(1, nx):
            acc += ry1[lax.rem(w.x + d, nx), x]
        s2[x, 4:8] = acc
    for d in range(1, chips):
        q, dev = chip(d)
        go(rcopy(s2.at[q], rx.at[xme], sd.at[d], qd.at[xme], dev))
    for d in range(1, chips):
        q, dev = chip(d)
        rcopy(rx.at[q], rx.at[q], sd.at[d], qd.at[q], dev).wait_recv()
    acc = s2[xme]
    for d in range(1, chips):
        acc += rx[lax.rem(xme + d, chips)]
    out[w.me] = acc
    sent = gather_start(w, out, se, qe)
    gather_wait(w, out, se, qe, sent)
    for r in range(3):
        pairs(r).wait_send()
    for cp in done:
        cp.wait_send()


def shards(dims, latent, noise, coef_state, coef_drift, coef_noise, step_index, table, gain, weight, rg):
    nt, ny, nx = dims
    nd = ny * nx
    chips = nt // 2
    per = 128 // nd
    half = per // 2
    dma = pltpu.SemaphoreType.DMA
    vmem = pltpu.VMEM
    field = (T, H, W, C)
    packed = (T, HP, W, AW)
    scratch = [
        vmem((2, HP, PW, C), F32),
        vmem((T, HP, PW, C), F32),
        vmem(field, F32),
        vmem(field, F32),
        vmem(field, F32),
        vmem(packed, BF16),
        vmem(packed, BF16),
        vmem(packed, BF16),
        vmem((3, AW, C), BF16),
        vmem((3, AW, C), BF16),
        vmem((T, C), F32),
        vmem((2 * T, C), F32),
        vmem((2 * T, C), F32),
        vmem((C, T * H * W), BF16),
        vmem((C, T * H * W), BF16),
    ]
    scratch += halo_scratch(2) + halo_scratch(T)
    scratch += gather_scratch(nd) * 3 + chain_scratch() * 3
    scratch += [
        vmem((chips, 2, 128, 8, 128), F32),
        vmem((chips, 128, 8, 128), F32),
        vmem((chips, ny, nx, per, 8, 128), F32),
        vmem((ny, chips, nx, half, 8, 128), F32),
        vmem((nx, chips, ny, half, 8, 128), F32),
        vmem((2, chips, max(nx, ny), half, 8, 128), F32),
        vmem((ny, chips, half, 8, 128), F32),
        vmem((nx, chips, half, 8, 128), F32),
        vmem((chips, per, 8, 128), F32),
        vmem((chips, per, 8, 128), F32),
    ]
    for count in (3, nx + ny, nx + ny, chips, nd):
        scratch += [dma((count,)), dma((count,))]
    traj, out = pl.pallas_call(
        functools.partial(k_all, dims),
        out_shape=(
            jax.ShapeDtypeStruct(field, F32),
            jax.ShapeDtypeStruct((nd, per, 8, 128), F32),
        ),
        in_specs=[SM] * 4 + [VM] * 6,
        out_specs=(VM, VM),
        scratch_shapes=scratch,
        compiler_params=pltpu.CompilerParams(
            vmem_limit_bytes=VLIM, collective_id=0, has_side_effects=True
        ),
        name="picard",
    )(step_index, coef_state, coef_drift, coef_noise, latent, rg, noise, weight, table, gain[None])
    tiles = out.reshape(128, 8, 128)[:120].reshape(3, 8, 40, 128)
    flat = jnp.transpose(tiles, (0, 2, 1, 3)).reshape(3, 40, AW)
    main = flat[:, :, 0:768].reshape(3, 40, 3, 256)
    tail = flat[:, :, 768:960].reshape(3, 40, 3, 64)
    grad = jnp.transpose(jnp.concatenate([main, tail], axis=3), (0, 2, 3, 1))
    return traj, grad


def solution(mesh):
    dims = (mesh.shape["tm"], mesh.shape["sy"], mesh.shape["sx"])
    tile = P("sy", "sx", None)
    full = P("tm", "sy", "sx", None)
    step = P("tm")
    return jax.shard_map(
        functools.partial(shards, dims),
        mesh=mesh,
        in_specs=(tile, full, step, step, step, step, P(), P(), P(), tile),
        out_specs=(full, P(None, None, None, "tm")),
        check_vma=False,
    )
```

```python
import functools

import jax
import jax.numpy as jnp
from jax import lax
from jax.experimental import pallas as pl
from jax.experimental.pallas import tpu as pltpu
from jax.sharding import PartitionSpec as P

MESH = pl.DeviceIdType.MESH
VM = pl.BlockSpec(memory_space=pltpu.VMEM)
SM = pl.BlockSpec(memory_space=pltpu.SMEM)
ANY = pl.BlockSpec(memory_space=pl.ANY)
F32 = jnp.float32
BF16 = jnp.bfloat16
HI = lax.Precision.HIGHEST
EPSILON = 1e-05
GSIZE = 10
T = 4
H = 16
W = 24
C = 320
PW = 32
HP = H + 2
AW = 1024
VLIM = 60 << 20


def rcopy(src, dst, ssem, rsem, dev):
    return pltpu.make_async_remote_copy(
        src_ref=src, dst_ref=dst, send_sem=ssem, recv_sem=rsem, device_id=dev, device_id_type=MESH
    )


def greet(devs):
    sem = pltpu.get_barrier_semaphore()
    for dev in devs:
        pl.semaphore_signal(sem, inc=1, device_id=dev, device_id_type=MESH)


class Where:
    def __init__(self, dims):
        self.nt, self.ny, self.nx = dims
        self.tm = lax.axis_index("tm")
        self.y = lax.axis_index("sy")
        self.x = lax.axis_index("sx")
        self.nd = self.ny * self.nx
        self.me = self.y * self.nx + self.x

    def dev(self, tm, y, x):
        return (tm, y, x)

    def tile(self, d):
        q = lax.rem(self.me + d, self.nd)
        return q, self.dev(self.tm, lax.div(q, self.nx), lax.rem(q, self.nx))

    def shift(self, dy, dx):
        return self.dev(
            self.tm,
            lax.rem(self.y + dy + self.ny, self.ny),
            lax.rem(self.x + dx + self.nx, self.nx),
        )

    def tiles(self):
        return [self.tile(d)[1] for d in range(1, self.nd)]

    def line(self):
        c = lax.rem(self.tm, 2)
        return [
            self.dev(self.tm + 1 - 2 * c, self.y, self.x),
            self.dev(lax.rem(self.tm + 2, self.nt), self.y, self.x),
            self.dev(lax.rem(self.tm + self.nt - 2, self.nt), self.y, self.x),
        ]


def gather_start(w, buf, ssem, rsem):
    out = []
    for d in range(1, w.nd):
        _, dev = w.tile(d)
        cp = rcopy(buf.at[w.me], buf.at[w.me], ssem.at[d], rsem.at[w.me], dev)
        cp.start()
        out.append(cp)
    return out


def gather_wait(w, buf, ssem, rsem, sent):
    for cp in sent:
        cp.wait_send()
    for d in range(1, w.nd):
        q, dev = w.tile(d)
        rcopy(buf.at[q], buf.at[q], ssem.at[d], rsem.at[q], dev).wait_recv()


def group_matrix():
    row = lax.broadcasted_iota(jnp.int32, (C, C), 0)
    col = lax.broadcasted_iota(jnp.int32, (C, C), 1)
    same = ((row * 6554) >> 16) == ((col * 6554) >> 16)
    return same.astype(F32)


def moments(buf, w):
    gm = group_matrix()
    n = float(H * W)
    both = buf[...]
    mean = jnp.sum(both[:, 0:T], axis=0) * (1.0 / w.nd)
    center = jnp.dot(mean, gm, precision=HI, preferred_element_type=F32) * (1.0 / GSIZE)
    off = both[:, 0:T] - center[None]
    dev = jnp.sum(both[:, T:] + n * off * off, axis=0)
    total = jnp.dot(dev, gm, precision=HI, preferred_element_type=F32)
    spread = total * (1.0 / (n * w.nd * GSIZE))
    return center, 1.0 / jnp.sqrt(spread + EPSILON)


SIDES = ((0, -1), (0, 1), (-1, 0), (1, 0), (-1, -1), (-1, 1), (1, -1), (1, 1))


def halo_pack(p, n, col_s, cor_s):
    for f in range(n):
        col_s[0, f] = p[f, 1 : 1 + H, 0, :]
        col_s[1, f] = p[f, 1 : 1 + H, W - 1, :]
        for j, (dy, dx) in enumerate(SIDES[4:]):
            row = 1 if dy < 0 else H
            lane = 0 if dx < 0 else W - 1
            cor_s[j, f : f + 1, :] = p[f, row, lane : lane + 1, :]


def halo_copies(w, p, col_s, col_r, cor_s, cor_r, ssem, rsem):
    out = []
    for j, (dy, dx) in enumerate(SIDES):
        dev = w.shift(dy, dx)
        if j < 2:
            src, dst = col_s.at[j], col_r.at[j]
        elif j < 4:
            row, land = (1, HP - 1) if dy < 0 else (H, 0)
            src, dst = p.at[:, row, 0:W, :], p.at[:, land, 0:W, :]
        else:
            src, dst = cor_s.at[j - 4], cor_r.at[j - 4]
        out.append(rcopy(src, dst, ssem.at[j], rsem.at[j], dev))
    return out


def halo_unpack(p, n, col_r, cor_r):
    for f in range(n):
        p[f, 1 : 1 + H, W, :] = col_r[0, f]
        p[f, 1 : 1 + H, PW - 1, :] = col_r[1, f]
        for j, (dy, dx) in enumerate(SIDES[4:]):
            row = HP - 1 if dy < 0 else 0
            lane = W if dx < 0 else PW - 1
            p[f, row, lane : lane + 1, :] = cor_r[j, f : f + 1, :]


def halo_scratch(n):
    return [
        pltpu.VMEM((2, n, H, C), F32),
        pltpu.VMEM((2, n, H, C), F32),
        pltpu.VMEM((4, 8, C), F32),
        pltpu.VMEM((4, 8, C), F32),
        pltpu.SemaphoreType.DMA((8,)),
        pltpu.SemaphoreType.DMA((8,)),
    ]


def gather_scratch(nd):
    return [
        pltpu.VMEM((nd, 8, C), F32),
        pltpu.SemaphoreType.DMA((nd,)),
        pltpu.SemaphoreType.DMA((nd,)),
    ]


def tile_moments(read, n):
    cells = 1.0 / (H * W)
    means, devs = [], []
    for f in range(n):

        def add(i, acc, f=f):
            return acc + read(f, i)

        total = lax.fori_loop(0, H, add, jnp.zeros((W, C), F32), unroll=4)
        mean = jnp.sum(total, axis=0, keepdims=True) * cells

        def add2(i, acc, f=f, mean=mean):
            v = read(f, i) - mean
            return acc + v * v

        total = lax.fori_loop(0, H, add2, jnp.zeros((W, C), F32), unroll=4)
        means.append(mean)
        devs.append(jnp.sum(total, axis=0, keepdims=True))
    return means, devs


CH = 4
ROWS = H // CH


def edge_mask(w, i):
    col = lax.broadcasted_iota(jnp.int32, (PW, 1), 0)
    rows = jnp.logical_and(
        jnp.logical_or(i > 0, w.y > 0), jnp.logical_or(i < HP - 1, w.y < w.ny - 1)
    )
    left = jnp.where(w.x > 0, 1, 0)
    right = jnp.where(w.x < w.nx - 1, 1, 0)
    inside = jnp.where(col == PW - 1, left, jnp.where(col == W, right, 1))
    return inside * jnp.where(rows, 1, 0) > 0


def pack_row(ab, k, i, v):
    shifts = [pltpu.roll(v, 1, 0)[0:W], v[0:W], pltpu.roll(v, PW - 1, 0)[0:W]]
    for s in range(3):
        ab[k, i, :, 256 * s : 256 * s + 256] = shifts[s][:, 0:256].astype(BF16)
    tail = jnp.concatenate(
        [u[:, 256:C] for u in shifts] + [jnp.zeros((W, 64), F32)], axis=1
    )
    ab[k, i, :, 768:AW] = tail.astype(BF16)


def conv_rows(ab, j, wt):
    acc = None
    for r in range(3):
        lhs = ab[:, pl.ds(ROWS * j + r, ROWS)].reshape(T * ROWS * W, AW)
        out = jnp.dot(lhs, wt[r], preferred_element_type=F32)
        acc = out if acc is None else acc + out
    return acc.reshape(T, ROWS, W, C)


def pack_forward(weight, wr):
    for r in range(3):
        wr[r, 960:AW] = jnp.zeros((64, C), BF16)
        for s in range(3):
            one = weight[r, s]
            wr[r, 256 * s : 256 * s + 256] = one[0:256]
            wr[r, 768 + 64 * s : 832 + 64 * s] = one[256:C]


def pack_backward(weight, wd):
    for r in range(3):
        wd[r, 960:AW] = jnp.zeros((64, C), BF16)
        for s in range(3):
            one = weight[2 - r, 2 - s].T
            wd[r, 256 * s : 256 * s + 256] = one[0:256]
            wd[r, 768 + 64 * s : 832 + 64 * s] = one[256:C]


def build_act(w, p, field, st, mod, ab, k):
    center = st[pl.ds(k, 1), :]
    inv = st[pl.ds(T + k, 1), :]
    m = mod[pl.ds(k, 1), :]

    def row(i, _):
        pre = (p[field, i] - center) * inv * m
        act = pre * (0.5 + 0.5 * jnp.tanh(0.5 * pre))
        act = jnp.where(edge_mask(w, i), act, 0.0)
        pack_row(ab, k, i, act)
        return 0

    lax.fori_loop(0, HP, row, 0, unroll=2)


def chain_scratch(count):
    part = (count, H // count // 2, W, C)
    return [
        pltpu.VMEM(part, F32),
        pltpu.VMEM(part, F32),
        pltpu.VMEM(part, F32),
        pltpu.VMEM(part, F32),
        pltpu.VMEM((H, W, C), F32),
        pltpu.SemaphoreType.DMA((3 * count,)),
        pltpu.SemaphoreType.DMA((3 * count,)),
    ]


class Chain:
    def __init__(self, w, total, scr, rev):
        self.w, self.total, self.scr = w, total, scr
        self.prx, self.inc, self.outc, self.offp, self.off, self.ss, self.rs = scr
        self.n = self.prx.shape[0]
        self.per = H // self.n
        self.c = lax.rem(w.tm, 2)
        self.chips = w.nt // 2
        x = lax.div(w.tm, 2)
        self.partner, nxt, prv = w.line()
        self.nxt = prv if rev else nxt
        self.x = self.chips - 1 - x if rev else x
        self.second = (self.c == 0) if rev else (self.c == 1)

    def rows(self, j, c):
        hh = self.per // 2
        return pl.ds(self.per * j + hh * c, hh)

    def pair(self, j):
        return rcopy(
            self.total.at[self.rows(j, 1 - self.c)], self.prx.at[j], self.ss.at[j], self.rs.at[j], self.partner
        )

    def fwd(self, j):
        return rcopy(
            self.outc.at[j], self.inc.at[j], self.ss.at[self.n + j], self.rs.at[self.n + j], self.nxt
        )

    def give(self, j, c):
        return rcopy(
            self.offp.at[j], self.off.at[self.rows(j, c)],
            self.ss.at[2 * self.n + j], self.rs.at[2 * self.n + j], self.partner,
        )

    def step(self, j):
        self.pair(j).wait_recv()

        @pl.when(self.x == 0)
        def _():
            self.inc[j] = jnp.zeros((self.per // 2, W, C), F32)

        @pl.when(self.x > 0)
        def _():
            self.fwd(j).wait_recv()

        mine = self.total[self.rows(j, self.c)]

        @pl.when(self.x < self.chips - 1)
        def _():
            self.outc[j] = self.inc[j] + (mine + self.prx[j])
            self.fwd(j).start()

        got = self.inc[j]
        self.off[self.rows(j, self.c)] = got + jnp.where(self.second, self.prx[j], 0.0)
        self.offp[j] = got + jnp.where(self.second, 0.0, mine)
        self.give(j, self.c).start()

    def some(self, low, high, cond):
        @pl.when(cond)
        def _():
            for j in range(low, high):
                self.step(j)

    def steps(self):
        for j in range(self.n):
            self.step(j)

    def finish(self):
        for j in range(self.n):
            self.pair(j).wait_send()
            self.give(j, self.c).wait_send()
            self.give(j, 1 - self.c).wait_recv()

            @pl.when(self.x < self.chips - 1)
            def _(j=j):
                self.fwd(j).wait_send()


DOTS = 3 * AW // 256
PARTS = 4
PART = DOTS // PARTS
TILES = 32


def wgrad(upt, ab, g, d, first):
    chips = g.shape[0]
    r, j = lax.div(d, 4), lax.rem(d, 4)
    lanes = pl.ds(pl.multiple_of(256 * j, 256), 256)
    rhs = [ab[k, pl.ds(r, H), :, lanes].reshape(H * W, 256) for k in range(T)]
    out = jnp.dot(upt[...], jnp.concatenate(rhs, axis=0), preferred_element_type=F32)
    h, base = lax.div(d, PART), 10 * lax.rem(d, PART)
    for half in range(2):
        place = pl.ds(base + 5 * half, 5)
        part = out[:, 128 * half : 128 * half + 128].reshape(chips, 2, 5, 8, 128)
        g[:, :, h, place] = part if first else g[:, :, h, place] + part


def loop_where(count, cond, step):
    def one(j, _):
        @pl.when(cond(j))
        def _():
            step(j, 0)

        return 0

    lax.fori_loop(0, count, one, 0)


def k_all(dims, *refs):
    (index, cstate, cdrift, cnoise, lat, rg, noise_h, weight_h, table_h, gain) = refs[:10]
    run_h, off_h, out = refs[10:13]
    (p, sp, run, run2, dact, ab1, ab2, abu, wr, wd, mod, st, st2, upt1, upt2) = refs[13:28]
    hal1, hal2 = refs[28:34], refs[34:40]
    gat1, gat2, gat3 = refs[40:43], refs[43:46], refs[46:49]
    ch1, ch2, ch3 = refs[49:56], refs[56:63], refs[63:70]
    g, ra, s, ry, rz, s1, rz1, ry1, s2, rx, fin = refs[70:81]
    noise, weight, table, local = refs[81:85]
    sems = refs[85:]
    sa, sb, sc_, sd, se = sems[0::2]
    qa, qb, qc, qd, qe = sems[1::2]
    w = Where(dims)
    chips = w.nt // 2
    c = lax.rem(w.tm, 2)
    xme = lax.div(w.tm, 2)
    ny, nx = w.ny, w.nx
    partner = w.line()[0]

    def chip(d):
        q = lax.rem(xme + d, chips)
        return q, w.dev(2 * q + c, w.y, w.x)

    devs = w.tiles() + [partner] + [chip(d)[1] for d in range(1, chips)]
    loads = [
        pltpu.make_async_copy(a, b, local.at[i])
        for i, (a, b) in enumerate(((weight_h, weight), (table_h, table), (noise_h, noise)))
    ]
    for cp in loads:
        cp.start()
    greet(devs)

    def fill(i, _):
        for f, ref in ((0, lat), (1, rg)):
            p[f, i + 1, 0:W, :] = ref[i]
        return 0

    lax.fori_loop(0, H, fill, 0)
    for hal in (hal1, hal2):
        hal[2][...] = jnp.zeros_like(hal[2])
    halo_pack(p, 2, hal1[0], hal1[2])
    means, vars_ = tile_moments(lambda f, i: lat[i], 1)
    gat1[0][w.me] = jnp.concatenate(means * T + vars_ * T, axis=0)
    pl.semaphore_wait(pltpu.get_barrier_semaphore(), len(devs))
    sent1 = gather_start(w, *gat1)
    copies1 = halo_copies(w, p, *hal1)
    for cp in copies1:
        cp.start()

    for cp in loads:
        cp.wait()
    pack_forward(weight, wr)
    step = lax.broadcasted_iota(jnp.int32, (1, table.shape[1]), 1)
    hot = jnp.concatenate([(step == index[k]).astype(F32) for k in range(T)] * 2, axis=0)
    rows = lax.dot_general(
        hot, table[...], (((1,), (1,)), ((), ())), precision=HI, preferred_element_type=F32
    )
    mod[...] = gain[...].reshape(1, C) * (1.0 + rows[0:T])
    gather_wait(w, *gat1, sent1)
    center, inv = moments(gat1[0], w)
    st[0:T] = center
    st[T:] = inv
    for cp in copies1:
        cp.wait()
    halo_unpack(p, 2, hal1[1], hal1[3])

    def prepare():
        pack_backward(weight, wd)
        turned = rg[...].reshape(H * W, C).T
        for k in range(T):
            upt2[:, k * H * W : (k + 1) * H * W] = (cdrift[k] * turned).astype(BF16)
        for h in range(PARTS):
            g[:, :, h, 10 * PART : TILES] = jnp.zeros((chips, 2, TILES - 10 * PART, 8, 128), F32)

        def up_row(i, _):
            v = jnp.where(edge_mask(w, i), p[1, i], 0.0)
            for k in range(T):
                pack_row(abu, k, i, cdrift[k] * v)
            return 0

        lax.fori_loop(0, HP, up_row, 0)

    def act1(k, _):
        build_act(w, p, 0, st, mod, ab1, k)
        return 0

    lax.fori_loop(0, T, act1, 0)
    chain1 = Chain(w, run.at[T - 1], ch1, False)
    chain3 = Chain(w, run2.at[T - 1], ch3, False)

    def sweep(field, ab, dst, j):
        conv = conv_rows(ab, j, wr)
        rows = pl.ds(ROWS * j, ROWS)
        acc = None
        for k in range(T):
            v = field(k, j)
            inc = cstate[k] * v + cdrift[k] * (v + conv[k])
            inc = inc + cnoise[k] * noise[k, rows].astype(F32)
            acc = inc if acc is None else acc + inc
            dst[k, rows] = acc

    for j in range(CH):
        sweep(lambda k, j: lat[pl.ds(ROWS * j, ROWS)], ab1, run, j)
        chain1.pair(2 * j).start()
        chain1.pair(2 * j + 1).start()
        if j > 0:
            chain1.some(2 * j - 2, 2 * j, chain1.x == 0)

    def back(j, _):
        dact[:, pl.ds(ROWS * j, ROWS)] = conv_rows(abu, j, wd)
        return 0

    early = jnp.where(xme >= chips - 1, CH, jnp.where(xme == chips - 2, 1, 0))
    pl.when(xme >= chips - 2)(prepare)
    loop_where(CH, lambda j: j < early, back)
    chain1.some(0, 2 * CH - 2, chain1.x > 0)
    chain1.some(2 * CH - 2, 2 * CH, chain1.x >= 0)
    chain1.finish()

    def states(i, _):
        base = lat[i]
        o = chain1.off[i]
        sp[0, i + 1, 0:W, :] = base + o
        for k in range(1, T):
            sp[k, i + 1, 0:W, :] = base + (o + run[k - 1, i])
        return 0

    lax.fori_loop(0, H, states, 0, unroll=2)
    halo_pack(sp, T, hal2[0], hal2[2])
    copies2 = halo_copies(w, sp, *hal2)
    for cp in copies2:
        cp.start()
    means, vars_ = tile_moments(lambda f, i: sp[f, i + 1, 0:W, :], T)
    gat2[0][w.me] = jnp.concatenate(means + vars_, axis=0)
    sent2 = gather_start(w, *gat2)
    pl.when(xme < chips - 2)(prepare)
    loop_where(CH, lambda j: j >= early, back)
    gather_wait(w, *gat2, sent2)
    center, inv = moments(gat2[0], w)
    st2[0:T] = center
    st2[T:] = inv

    sums = []
    for k in range(T):
        center, inv, m = st2[k : k + 1, :], st2[T + k : T + k + 1, :], mod[k : k + 1, :]

        def dnorm(i, acc, k=k, center=center, inv=inv, m=m):
            plain, cross = acc
            norm = (sp[k, i + 1, 0:W, :] - center) * inv
            pre = norm * m
            sig = 0.5 + 0.5 * jnp.tanh(0.5 * pre)
            d = dact[k, i] * sig * (1.0 + pre * (1.0 - sig)) * m
            dact[k, i] = d
            return plain + d, cross + d * norm

        zero = jnp.zeros((W, C), F32)
        plain, cross = lax.fori_loop(0, H, dnorm, (zero, zero), unroll=2)
        sums.append((jnp.sum(plain, axis=0, keepdims=True), jnp.sum(cross, axis=0, keepdims=True)))
    gat3[0][w.me] = jnp.concatenate([a for a, _ in sums] + [b for _, b in sums], axis=0)
    sent3 = gather_start(w, *gat3)
    for cp in copies2:
        cp.wait()
    halo_unpack(sp, T, hal2[1], hal2[3])

    def act2(k, _):
        build_act(w, sp, k, st2, mod, ab2, k)
        return 0

    lax.fori_loop(0, T, act2, 0)
    gather_wait(w, *gat3, sent3)
    sums = jnp.sum(gat3[0][...], axis=0)
    means = jnp.dot(sums, group_matrix(), precision=HI, preferred_element_type=F32)
    means = means * (1.0 / (H * W * w.nd * GSIZE))

    chain2 = Chain(w, run.at[0], ch2, True)

    def through(i, _):
        rgv = rg[i]
        acc = None
        for k in range(T - 1, -1, -1):
            center, inv = st2[k : k + 1, :], st2[T + k : T + k + 1, :]
            plain, cross = means[k : k + 1, :], means[T + k : T + k + 1, :]
            norm = (sp[k, i + 1, 0:W, :] - center) * inv
            d = (dact[k, i] - plain - norm * cross) * inv
            t = cstate[k] * rgv + (cdrift[k] * rgv + d)
            acc = t if acc is None else acc + t
            run[k, i] = acc
        return 0

    for j in range(CH):
        lax.fori_loop(0, ROWS, lambda i, z, j=j: through(ROWS * j + i, z), 0)
        chain2.pair(2 * j).start()
        chain2.pair(2 * j + 1).start()

    def second(j, _):
        sweep(lambda k, j: sp[k, pl.ds(1 + ROWS * j, ROWS), 0:W, :], ab2, run2, j)
        return 0

    def weight2(d, _):
        wgrad(upt2, ab2, g, d, True)
        return 0

    n = jnp.clip(2 * chain2.x, 0, CH)
    m = jnp.where(chain2.x == chips - 1, DOTS, 0)
    loop_where(CH, lambda j: j < n, second)
    loop_where(DOTS, lambda d: d < m, weight2)
    chain2.steps()
    loop_where(CH, lambda j: j >= n, second)
    for j in range(CH):
        chain3.pair(j).start()
    store = pltpu.make_async_copy(run2, run_h, local.at[3])
    store.start()
    loop_where(DOTS, lambda d: d >= m, weight2)
    chain2.finish()
    chain3.some(0, CH, chain3.x == 0)

    for k in range(T):
        adj = chain2.off[...] + run[k + 1] if k + 1 < T else chain2.off[...]
        up = (cdrift[k] * adj).reshape(H * W, C).astype(BF16)
        upt1[:, k * H * W : (k + 1) * H * W] = up.T

    def pairs(h):
        return rcopy(g.at[:, 1 - c, h], ra.at[h], sa.at[h], qa.at[h], partner)

    done = []

    def go(cp):
        cp.start()
        done.append(cp)

    def weight1(d, _):
        wgrad(upt1, ab1, g, d, False)
        return 0

    per = s.shape[4]
    two = per // 2

    def add(h):
        pairs(h).wait_recv()

        def one(q, _):
            place = pl.ds(per * q, per)
            for x in range(chips):
                s[h, x, lax.div(q, nx), lax.rem(q, nx)] = g[x, c, h, place] + ra[h, x, place]
            return 0

        lax.fori_loop(0, w.nd, one, 0)

    def along(h):
        b = h * (nx + ny)
        for d in range(1, nx):
            q = lax.rem(w.x + d, nx)
            go(rcopy(s.at[h, :, :, q, 0:two], rz.at[h, w.x], sb.at[b + d], qb.at[b + w.x], w.shift(0, d)))
        for d in range(1, ny):
            q = lax.rem(w.y + d, ny)
            b2 = b + nx
            go(rcopy(s.at[h, :, q, :, two:per], ry.at[h, w.y], sb.at[b2 + d], qb.at[b2 + w.y], w.shift(d, 0)))

    def across(h):
        b = h * (nx + ny)
        for d in range(1, nx):
            q = lax.rem(w.x + d, nx)
            rcopy(rz.at[h, q], rz.at[h, q], sb.at[b + d], qb.at[b + q], partner).wait_recv()
        for d in range(1, ny):
            q = lax.rem(w.y + d, ny)
            b2 = b + nx
            rcopy(ry.at[h, q], ry.at[h, q], sb.at[b2 + d], qb.at[b2 + q], partner).wait_recv()

        def join(x, _):
            for i in range(ny):
                acc = s[h, x, i, w.x, 0:two]
                for d in range(1, nx):
                    acc += rz[h, lax.rem(w.x + d, nx), x, i]
                s1[h, 0, x, i] = acc
            for j in range(nx):
                acc = s[h, x, w.y, j, two:per]
                for d in range(1, ny):
                    acc += ry[h, lax.rem(w.y + d, ny), x, j]
                s1[h, 1, x, j] = acc
            return 0

        lax.fori_loop(0, chips, join, 0)
        b = h * (nx + ny)
        for d in range(1, ny):
            q = lax.rem(w.y + d, ny)
            go(rcopy(s1.at[h, 0, :, q], rz1.at[h, w.y], sc_.at[b + d], qc.at[b + w.y], w.shift(d, 0)))
        for d in range(1, nx):
            q = lax.rem(w.x + d, nx)
            b2 = b + ny
            go(rcopy(s1.at[h, 1, :, q], ry1.at[h, w.x], sc_.at[b2 + d], qc.at[b2 + w.x], w.shift(0, d)))

    def chips_out(h):
        b = h * (nx + ny)
        for d in range(1, ny):
            q = lax.rem(w.y + d, ny)
            rcopy(rz1.at[h, q], rz1.at[h, q], sc_.at[b + d], qc.at[b + q], partner).wait_recv()
        for d in range(1, nx):
            q = lax.rem(w.x + d, nx)
            b2 = b + ny
            rcopy(ry1.at[h, q], ry1.at[h, q], sc_.at[b2 + d], qc.at[b2 + q], partner).wait_recv()
        for x in range(chips):
            acc = s1[h, 0, x, w.y]
            for d in range(1, ny):
                acc += rz1[h, lax.rem(w.y + d, ny), x]
            s2[h, x, 0:two] = acc
            acc = s1[h, 1, x, w.x]
            for d in range(1, nx):
                acc += ry1[h, lax.rem(w.x + d, nx), x]
            s2[h, x, two:per] = acc
        for d in range(1, chips):
            q, dev = chip(d)
            go(rcopy(s2.at[h, q], rx.at[h, xme], sd.at[h * chips + d], qd.at[h * chips + xme], dev))

    def spread(h):
        for d in range(1, chips):
            q, dev = chip(d)
            rcopy(rx.at[h, q], rx.at[h, q], sd.at[h * chips + d], qd.at[h * chips + q], dev).wait_recv()
        acc = s2[h, xme]
        for d in range(1, chips):
            acc += rx[h, lax.rem(xme + d, chips)]
        fin[h, w.me] = acc
        b = pl.ds(h * w.nd, w.nd)
        return gather_start(w, fin.at[h], se.at[b], qe.at[b])

    for h in range(PARTS):
        lax.fori_loop(PART * h, PART * h + PART, weight1, 0)
        pairs(h).start()
        if h > 1:
            add(h - 2)
            along(h - 2)
    for h in (PARTS - 2, PARTS - 1):
        add(h)
        along(h)
    chain3.some(0, CH, chain3.x == 1)
    across(0)
    across(1)
    chain3.some(0, CH, chain3.x == 2)
    across(2)
    chips_out(0)
    chips_out(1)
    across(3)
    sent = [spread(0), spread(1)]
    chips_out(2)
    chain3.some(0, CH, chain3.x == chips - 1)
    chips_out(3)
    sent += [spread(2), spread(3)]
    chain3.finish()
    store2 = pltpu.make_async_copy(chain3.off, off_h, local.at[4])
    store2.start()
    for h in range(PARTS):
        b = pl.ds(h * w.nd, w.nd)
        gather_wait(w, fin.at[h], se.at[b], qe.at[b], sent[h])
    for r in range(3):
        cols = []
        for l in range(8):
            d = 4 * r + l // 2
            first_tile = 10 * (d % PART) + 5 * (l % 2)
            tiles = [fin[d // PART, t // per, t % per] for t in range(first_tile, first_tile + 5)]
            cols.append(jnp.concatenate(tiles, axis=0))
        whole = jnp.concatenate(cols, axis=1)
        for q in range(3):
            out[r, q, :, 0:256] = whole[:, 256 * q : 256 * q + 256]
            out[r, q, :, 256:C] = whole[:, 768 + 64 * q : 832 + 64 * q]
    store.wait()
    store2.wait()
    for h in range(PARTS):
        pairs(h).wait_send()
    for cp in done:
        cp.wait_send()


def shards(dims, latent, noise, coef_state, coef_drift, coef_noise, step_index, table, gain, weight, rg):
    nt, ny, nx = dims
    nd = ny * nx
    chips = nt // 2
    per = TILES // nd
    half = per // 2
    dma = pltpu.SemaphoreType.DMA
    vmem = pltpu.VMEM
    field = (T, H, W, C)
    packed = (T, HP, W, AW)
    scratch = [
        vmem((2, HP, PW, C), F32),
        vmem((T, HP, PW, C), F32),
        vmem(field, F32),
        vmem(field, F32),
        vmem(field, F32),
        vmem(packed, BF16),
        vmem(packed, BF16),
        vmem(packed, BF16),
        vmem((3, AW, C), BF16),
        vmem((3, AW, C), BF16),
        vmem((T, C), F32),
        vmem((2 * T, C), F32),
        vmem((2 * T, C), F32),
        vmem((C, T * H * W), BF16),
        vmem((C, T * H * W), BF16),
    ]
    scratch += halo_scratch(2) + halo_scratch(T)
    scratch += gather_scratch(nd) * 3 + chain_scratch(2 * CH) * 2 + chain_scratch(CH)
    scratch += [
        vmem((chips, 2, PARTS, TILES, 8, 128), F32),
        vmem((PARTS, chips, TILES, 8, 128), F32),
        vmem((PARTS, chips, ny, nx, per, 8, 128), F32),
        vmem((PARTS, ny, chips, nx, half, 8, 128), F32),
        vmem((PARTS, nx, chips, ny, half, 8, 128), F32),
        vmem((PARTS, 2, chips, max(nx, ny), half, 8, 128), F32),
        vmem((PARTS, ny, chips, half, 8, 128), F32),
        vmem((PARTS, nx, chips, half, 8, 128), F32),
        vmem((PARTS, chips, per, 8, 128), F32),
        vmem((PARTS, chips, per, 8, 128), F32),
        vmem((PARTS, nd, per, 8, 128), F32),
        vmem(noise.shape, BF16),
        vmem(weight.shape, BF16),
        vmem(table.shape[::-1], F32),
        dma((5,)),
    ]
    for count in (1, nx + ny, nx + ny, chips, nd):
        scratch += [dma((PARTS * count,)), dma((PARTS * count,))]
    run, off, out = pl.pallas_call(
        functools.partial(k_all, dims),
        out_shape=(
            jax.ShapeDtypeStruct(field, F32),
            jax.ShapeDtypeStruct((H, W, C), F32),
            jax.ShapeDtypeStruct((3, 3, C // nt, C), F32),
        ),
        in_specs=[SM] * 4 + [VM] * 2 + [ANY] * 3 + [VM],
        out_specs=(ANY, ANY, VM),
        scratch_shapes=scratch,
        compiler_params=pltpu.CompilerParams(
            vmem_limit_bytes=VLIM, collective_id=0, has_side_effects=True
        ),
        name="picard",
    )(step_index, coef_state, coef_drift, coef_noise, latent, rg, noise, weight, table.T, gain)
    traj = latent[None] + (off[None] + run)
    return traj, jnp.transpose(out, (0, 1, 3, 2))


def solution(mesh):
    dims = (mesh.shape["tm"], mesh.shape["sy"], mesh.shape["sx"])
    tile = P("sy", "sx", None)
    full = P("tm", "sy", "sx", None)
    step = P("tm")
    return jax.shard_map(
        functools.partial(shards, dims),
        mesh=mesh,
        in_specs=(tile, full, step, step, step, step, P(), P(), P(), tile),
        out_specs=(full, P(None, None, None, "tm")),
        check_vma=False,
    )
```

```python
import functools

import jax
import jax.numpy as jnp
from jax import lax
from jax.experimental import pallas as pl
from jax.experimental.pallas import tpu as pltpu
from jax.sharding import PartitionSpec as P

MESH = pl.DeviceIdType.MESH
VM = pl.BlockSpec(memory_space=pltpu.VMEM)
SM = pl.BlockSpec(memory_space=pltpu.SMEM)
ANY = pl.BlockSpec(memory_space=pl.ANY)
F32 = jnp.float32
BF16 = jnp.bfloat16
HI = lax.Precision.HIGHEST
EPSILON = 1e-05
GSIZE = 10
T = 4
H = 16
W = 24
C = 320
PW = 32
HP = H + 2
AW = 1024
VLIM = 60 << 20


def rcopy(src, dst, ssem, rsem, dev):
    return pltpu.make_async_remote_copy(
        src_ref=src, dst_ref=dst, send_sem=ssem, recv_sem=rsem, device_id=dev, device_id_type=MESH
    )


def greet(devs):
    sem = pltpu.get_barrier_semaphore()
    for dev in devs:
        pl.semaphore_signal(sem, inc=1, device_id=dev, device_id_type=MESH)


class Where:
    def __init__(self, dims):
        self.nt, self.ny, self.nx = dims
        self.tm = lax.axis_index("tm")
        self.y = lax.axis_index("sy")
        self.x = lax.axis_index("sx")
        self.nd = self.ny * self.nx
        self.me = self.y * self.nx + self.x

    def dev(self, tm, y, x):
        return (tm, y, x)

    def tile(self, d):
        q = lax.rem(self.me + d, self.nd)
        return q, self.dev(self.tm, lax.div(q, self.nx), lax.rem(q, self.nx))

    def shift(self, dy, dx):
        return self.dev(
            self.tm,
            lax.rem(self.y + dy + self.ny, self.ny),
            lax.rem(self.x + dx + self.nx, self.nx),
        )

    def tiles(self):
        return [self.tile(d)[1] for d in range(1, self.nd)]

    def line(self):
        c = lax.rem(self.tm, 2)
        return [
            self.dev(self.tm + 1 - 2 * c, self.y, self.x),
            self.dev(lax.rem(self.tm + 2, self.nt), self.y, self.x),
            self.dev(lax.rem(self.tm + self.nt - 2, self.nt), self.y, self.x),
        ]


def gather_start(w, buf, ssem, rsem):
    out = []
    for d in range(1, w.nd):
        _, dev = w.tile(d)
        cp = rcopy(buf.at[w.me], buf.at[w.me], ssem.at[d], rsem.at[w.me], dev)
        cp.start()
        out.append(cp)
    return out


def gather_wait(w, buf, ssem, rsem, sent):
    for cp in sent:
        cp.wait_send()
    for d in range(1, w.nd):
        q, dev = w.tile(d)
        rcopy(buf.at[q], buf.at[q], ssem.at[d], rsem.at[q], dev).wait_recv()


def group_matrix():
    row = lax.broadcasted_iota(jnp.int32, (C, C), 0)
    col = lax.broadcasted_iota(jnp.int32, (C, C), 1)
    same = ((row * 6554) >> 16) == ((col * 6554) >> 16)
    return same.astype(F32)


def moments(buf, w):
    gm = group_matrix()
    n = float(H * W)
    both = buf[...]
    mean = jnp.sum(both[:, 0:T], axis=0) * (1.0 / w.nd)
    center = jnp.dot(mean, gm, precision=HI, preferred_element_type=F32) * (1.0 / GSIZE)
    off = both[:, 0:T] - center[None]
    dev = jnp.sum(both[:, T:] + n * off * off, axis=0)
    total = jnp.dot(dev, gm, precision=HI, preferred_element_type=F32)
    spread = total * (1.0 / (n * w.nd * GSIZE))
    return center, 1.0 / jnp.sqrt(spread + EPSILON)


SIDES = ((0, -1), (0, 1), (-1, 0), (1, 0), (-1, -1), (-1, 1), (1, -1), (1, 1))


def halo_pack(p, n, col_s, cor_s):
    for f in range(n):
        col_s[0, f] = p[f, 1 : 1 + H, 0, :]
        col_s[1, f] = p[f, 1 : 1 + H, W - 1, :]
        for j, (dy, dx) in enumerate(SIDES[4:]):
            row = 1 if dy < 0 else H
            lane = 0 if dx < 0 else W - 1
            cor_s[j, f : f + 1, :] = p[f, row, lane : lane + 1, :]


def halo_copies(w, p, col_s, col_r, cor_s, cor_r, ssem, rsem):
    out = []
    for j, (dy, dx) in enumerate(SIDES):
        dev = w.shift(dy, dx)
        if j < 2:
            src, dst = col_s.at[j], col_r.at[j]
        elif j < 4:
            row, land = (1, HP - 1) if dy < 0 else (H, 0)
            src, dst = p.at[:, row, 0:W, :], p.at[:, land, 0:W, :]
        else:
            src, dst = cor_s.at[j - 4], cor_r.at[j - 4]
        out.append(rcopy(src, dst, ssem.at[j], rsem.at[j], dev))
    return out


def halo_unpack(p, n, col_r, cor_r):
    for f in range(n):
        p[f, 1 : 1 + H, W, :] = col_r[0, f]
        p[f, 1 : 1 + H, PW - 1, :] = col_r[1, f]
        for j, (dy, dx) in enumerate(SIDES[4:]):
            row = HP - 1 if dy < 0 else 0
            lane = W if dx < 0 else PW - 1
            p[f, row, lane : lane + 1, :] = cor_r[j, f : f + 1, :]


def halo_scratch(n):
    return [
        pltpu.VMEM((2, n, H, C), F32),
        pltpu.VMEM((2, n, H, C), F32),
        pltpu.VMEM((4, 8, C), F32),
        pltpu.VMEM((4, 8, C), F32),
        pltpu.SemaphoreType.DMA((8,)),
        pltpu.SemaphoreType.DMA((8,)),
    ]


def gather_scratch(nd):
    return [
        pltpu.VMEM((nd, 8, C), F32),
        pltpu.SemaphoreType.DMA((nd,)),
        pltpu.SemaphoreType.DMA((nd,)),
    ]


def tile_moments(read, n):
    cells = 1.0 / (H * W)
    means, devs = [], []
    for f in range(n):

        def add(i, acc, f=f):
            return acc + read(f, i)

        total = lax.fori_loop(0, H, add, jnp.zeros((W, C), F32), unroll=4)
        mean = jnp.sum(total, axis=0, keepdims=True) * cells

        def add2(i, acc, f=f, mean=mean):
            v = read(f, i) - mean
            return acc + v * v

        total = lax.fori_loop(0, H, add2, jnp.zeros((W, C), F32), unroll=4)
        means.append(mean)
        devs.append(jnp.sum(total, axis=0, keepdims=True))
    return means, devs


CH = 4
ROWS = H // CH


def edge_mask(w, i):
    col = lax.broadcasted_iota(jnp.int32, (PW, 1), 0)
    rows = jnp.logical_and(
        jnp.logical_or(i > 0, w.y > 0), jnp.logical_or(i < HP - 1, w.y < w.ny - 1)
    )
    left = jnp.where(w.x > 0, 1, 0)
    right = jnp.where(w.x < w.nx - 1, 1, 0)
    inside = jnp.where(col == PW - 1, left, jnp.where(col == W, right, 1))
    return inside * jnp.where(rows, 1, 0) > 0


def pack_row(ab, k, i, v):
    shifts = [pltpu.roll(v, 1, 0)[0:W], v[0:W], pltpu.roll(v, PW - 1, 0)[0:W]]
    for s in range(3):
        ab[k, i, :, 256 * s : 256 * s + 256] = shifts[s][:, 0:256].astype(BF16)
    tail = jnp.concatenate(
        [u[:, 256:C] for u in shifts] + [jnp.zeros((W, 64), F32)], axis=1
    )
    ab[k, i, :, 768:AW] = tail.astype(BF16)


def conv_rows(ab, j, wt):
    acc = None
    for r in range(3):
        lhs = ab[:, pl.ds(ROWS * j + r, ROWS)].reshape(T * ROWS * W, AW)
        out = jnp.dot(lhs, wt[r], preferred_element_type=F32)
        acc = out if acc is None else acc + out
    return acc.reshape(T, ROWS, W, C)


def pack_forward(weight, wr):
    for r in range(3):
        wr[r, 960:AW] = jnp.zeros((64, C), BF16)
        for s in range(3):
            one = weight[r, s]
            wr[r, 256 * s : 256 * s + 256] = one[0:256]
            wr[r, 768 + 64 * s : 832 + 64 * s] = one[256:C]


def pack_backward(weight, wd):
    for r in range(3):
        wd[r, 960:AW] = jnp.zeros((64, C), BF16)
        for s in range(3):
            one = weight[2 - r, 2 - s].T
            wd[r, 256 * s : 256 * s + 256] = one[0:256]
            wd[r, 768 + 64 * s : 832 + 64 * s] = one[256:C]


def build_act(w, p, field, st, mod, ab, k):
    center = st[pl.ds(k, 1), :]
    inv = st[pl.ds(T + k, 1), :]
    m = mod[pl.ds(k, 1), :]

    def row(i, _):
        pre = (p[field, i] - center) * inv * m
        act = pre * (0.5 + 0.5 * jnp.tanh(0.5 * pre))
        act = jnp.where(edge_mask(w, i), act, 0.0)
        pack_row(ab, k, i, act)
        return 0

    lax.fori_loop(0, HP, row, 0, unroll=2)


def chain_scratch(count):
    part = (count, H // count // 2, W, C)
    return [
        pltpu.VMEM(part, F32),
        pltpu.VMEM(part, F32),
        pltpu.VMEM(part, F32),
        pltpu.VMEM(part, F32),
        pltpu.VMEM((H, W, C), F32),
        pltpu.SemaphoreType.DMA((3 * count,)),
        pltpu.SemaphoreType.DMA((3 * count,)),
    ]


class Chain:
    def __init__(self, w, total, scr, rev):
        self.w, self.total, self.scr = w, total, scr
        self.prx, self.inc, self.outc, self.offp, self.off, self.ss, self.rs = scr
        self.n = self.prx.shape[0]
        self.per = H // self.n
        self.c = lax.rem(w.tm, 2)
        self.chips = w.nt // 2
        x = lax.div(w.tm, 2)
        self.partner, nxt, prv = w.line()
        self.nxt = prv if rev else nxt
        self.x = self.chips - 1 - x if rev else x
        self.second = (self.c == 0) if rev else (self.c == 1)

    def rows(self, j, c):
        hh = self.per // 2
        return pl.ds(self.per * j + hh * c, hh)

    def pair(self, j):
        return rcopy(
            self.total.at[self.rows(j, 1 - self.c)], self.prx.at[j], self.ss.at[j], self.rs.at[j], self.partner
        )

    def fwd(self, j):
        return rcopy(
            self.outc.at[j], self.inc.at[j], self.ss.at[self.n + j], self.rs.at[self.n + j], self.nxt
        )

    def give(self, j, c):
        return rcopy(
            self.offp.at[j], self.off.at[self.rows(j, c)],
            self.ss.at[2 * self.n + j], self.rs.at[2 * self.n + j], self.partner,
        )

    def step(self, j):
        self.pair(j).wait_recv()

        @pl.when(self.x == 0)
        def _():
            self.inc[j] = jnp.zeros((self.per // 2, W, C), F32)

        @pl.when(self.x > 0)
        def _():
            self.fwd(j).wait_recv()

        mine = self.total[self.rows(j, self.c)]

        @pl.when(self.x < self.chips - 1)
        def _():
            self.outc[j] = self.inc[j] + (mine + self.prx[j])
            self.fwd(j).start()

        got = self.inc[j]
        self.off[self.rows(j, self.c)] = got + jnp.where(self.second, self.prx[j], 0.0)
        self.offp[j] = got + jnp.where(self.second, 0.0, mine)
        self.give(j, self.c).start()

    def some(self, low, high, cond):
        @pl.when(cond)
        def _():
            for j in range(low, high):
                self.step(j)

    def steps(self):
        for j in range(self.n):
            self.step(j)

    def finish(self):
        for j in range(self.n):
            self.pair(j).wait_send()
            self.give(j, self.c).wait_send()
            self.give(j, 1 - self.c).wait_recv()

            @pl.when(self.x < self.chips - 1)
            def _(j=j):
                self.fwd(j).wait_send()


DOTS = 3 * AW // 256
PARTS = 4
PART = DOTS // PARTS
TILES = 32


def wgrad(upt, ab, g, d, first):
    chips = g.shape[0]
    r, j = lax.div(d, 4), lax.rem(d, 4)
    lanes = pl.ds(pl.multiple_of(256 * j, 256), 256)
    rhs = [ab[k, pl.ds(r, H), :, lanes].reshape(H * W, 256) for k in range(T)]
    out = jnp.dot(upt[...], jnp.concatenate(rhs, axis=0), preferred_element_type=F32)
    h, base = lax.div(d, PART), 10 * lax.rem(d, PART)
    for half in range(2):
        place = pl.ds(base + 5 * half, 5)
        part = out[:, 128 * half : 128 * half + 128].reshape(chips, 2, 5, 8, 128)
        g[:, :, h, place] = part if first else g[:, :, h, place] + part


def loop_where(count, cond, step):
    def one(j, _):
        @pl.when(cond(j))
        def _():
            step(j, 0)

        return 0

    lax.fori_loop(0, count, one, 0)


def k_all(dims, *refs):
    (index, cstate, cdrift, cnoise, lat_h, rg_h, noise_h, weight_h, table_h, gain) = refs[:10]
    run_h, off_h, out = refs[10:13]
    (p, sp, run, run2, dact, ab1, ab2, abu, wr, wd, mod, st, st2, upt1, upt2) = refs[13:28]
    hal1, hal2 = refs[28:34], refs[34:40]
    gat1, gat2, gat3 = refs[40:43], refs[43:46], refs[46:49]
    ch1, ch2, ch3 = refs[49:56], refs[56:63], refs[63:70]
    g, ra, s, ry, rz, s1, rz1, ry1, s2, rx, fin = refs[70:81]
    noise, weight, table, lat, rg, sx, rf, local = refs[81:89]
    sems = refs[89:]
    sa, sb, sc_, sd, se, sf = sems[0::2]
    qa, qb, qc, qd, qe, qf = sems[1::2]
    w = Where(dims)
    chips = w.nt // 2
    c = lax.rem(w.tm, 2)
    xme = lax.div(w.tm, 2)
    ny, nx = w.ny, w.nx
    partner = w.line()[0]

    def chip(d):
        q = lax.rem(xme + d, chips)
        return q, w.dev(2 * q + c, w.y, w.x)

    devs = w.tiles() + [partner] + [chip(d)[1] for d in range(1, chips)]
    loads = [
        pltpu.make_async_copy(a, b, local.at[i])
        for i, (a, b) in enumerate(((lat_h, lat), (rg_h, rg), (weight_h, weight), (table_h, table), (noise_h, noise)))
    ]
    for cp in loads:
        cp.start()
    greet(devs)
    for cp in loads[:2]:
        cp.wait()

    def fill(i, _):
        for f, ref in ((0, lat), (1, rg)):
            p[f, i + 1, 0:W, :] = ref[i]
        return 0

    lax.fori_loop(0, H, fill, 0)
    for hal in (hal1, hal2):
        hal[2][...] = jnp.zeros_like(hal[2])
    halo_pack(p, 2, hal1[0], hal1[2])
    means, vars_ = tile_moments(lambda f, i: lat[i], 1)
    gat1[0][w.me] = jnp.concatenate(means * T + vars_ * T, axis=0)
    pl.semaphore_wait(pltpu.get_barrier_semaphore(), len(devs))
    sent1 = gather_start(w, *gat1)
    copies1 = halo_copies(w, p, *hal1)
    for cp in copies1:
        cp.start()

    for cp in loads[2:]:
        cp.wait()
    pack_forward(weight, wr)
    step = lax.broadcasted_iota(jnp.int32, (1, table.shape[1]), 1)
    hot = jnp.concatenate([(step == index[k]).astype(F32) for k in range(T)] * 2, axis=0)
    rows = lax.dot_general(
        hot, table[...], (((1,), (1,)), ((), ())), precision=HI, preferred_element_type=F32
    )
    mod[...] = gain[...].reshape(1, C) * (1.0 + rows[0:T])
    gather_wait(w, *gat1, sent1)
    center, inv = moments(gat1[0], w)
    st[0:T] = center
    st[T:] = inv
    for cp in copies1:
        cp.wait()
    halo_unpack(p, 2, hal1[1], hal1[3])

    def prepare():
        pack_backward(weight, wd)
        turned = rg[...].reshape(H * W, C).T
        for k in range(T):
            upt2[:, k * H * W : (k + 1) * H * W] = (cdrift[k] * turned).astype(BF16)
        for h in range(PARTS):
            g[:, :, h, 10 * PART : TILES] = jnp.zeros((chips, 2, TILES - 10 * PART, 8, 128), F32)

        def up_row(i, _):
            v = jnp.where(edge_mask(w, i), p[1, i], 0.0)
            for k in range(T):
                pack_row(abu, k, i, cdrift[k] * v)
            return 0

        lax.fori_loop(0, HP, up_row, 0)

    def act_row(i):
        center, inv = st[0:1, :], st[T : T + 1, :]
        norm = (p[0, i] - center) * inv
        mask = edge_mask(w, i)
        for k in range(T):
            pre = norm * mod[k : k + 1, :]
            act = pre * (0.5 + 0.5 * jnp.tanh(0.5 * pre))
            pack_row(ab1, k, i, jnp.where(mask, act, 0.0))

    def act1(i, _):
        act_row(i)
        return 0

    lax.fori_loop(0, ROWS + 2, act1, 0)
    chain1 = Chain(w, run.at[T - 1], ch1, False)
    chain3 = Chain(w, run2.at[T - 1], ch3, False)

    def sweep(field, ab, dst, j):
        conv = conv_rows(ab, j, wr)
        rows = pl.ds(ROWS * j, ROWS)
        acc = None
        for k in range(T):
            v = field(k, j)
            inc = cstate[k] * v + cdrift[k] * (v + conv[k])
            inc = inc + cnoise[k] * noise[k, rows].astype(F32)
            acc = inc if acc is None else acc + inc
            dst[k, rows] = acc

    for j in range(CH):
        if j + 1 < CH:
            for i in range(ROWS):
                act_row(ROWS * (j + 1) + 2 + i)
        sweep(lambda k, j: lat[pl.ds(ROWS * j, ROWS)], ab1, run, j)
        chain1.pair(2 * j).start()
        chain1.pair(2 * j + 1).start()
        if j > 0:
            chain1.some(2 * j - 2, 2 * j, chain1.x == 0)

    def back(j, _):
        dact[:, pl.ds(ROWS * j, ROWS)] = conv_rows(abu, j, wd)
        return 0

    early = jnp.where(xme >= chips - 1, CH, jnp.where(xme == chips - 2, 1, 0))
    pl.when(xme >= chips - 2)(prepare)
    loop_where(CH, lambda j: j < early, back)
    chain1.some(0, 2 * CH - 2, chain1.x > 0)
    chain1.some(2 * CH - 2, 2 * CH, chain1.x >= 0)
    chain1.finish()

    def states(i, _):
        base = lat[i]
        o = chain1.off[i]
        sp[0, i + 1, 0:W, :] = base + o
        for k in range(1, T):
            sp[k, i + 1, 0:W, :] = base + (o + run[k - 1, i])
        return 0

    lax.fori_loop(0, H, states, 0, unroll=2)
    halo_pack(sp, T, hal2[0], hal2[2])
    copies2 = halo_copies(w, sp, *hal2)
    for cp in copies2:
        cp.start()
    means, vars_ = tile_moments(lambda f, i: sp[f, i + 1, 0:W, :], T)
    gat2[0][w.me] = jnp.concatenate(means + vars_, axis=0)
    sent2 = gather_start(w, *gat2)
    pl.when(xme < chips - 2)(prepare)
    loop_where(CH, lambda j: j >= early, back)
    gather_wait(w, *gat2, sent2)
    center, inv = moments(gat2[0], w)
    st2[0:T] = center
    st2[T:] = inv

    sums = []
    for k in range(T):
        center, inv, m = st2[k : k + 1, :], st2[T + k : T + k + 1, :], mod[k : k + 1, :]

        def dnorm(i, acc, k=k, center=center, inv=inv, m=m):
            plain, cross = acc
            norm = (sp[k, i + 1, 0:W, :] - center) * inv
            pre = norm * m
            sig = 0.5 + 0.5 * jnp.tanh(0.5 * pre)
            d = dact[k, i] * sig * (1.0 + pre * (1.0 - sig)) * m
            dact[k, i] = d
            return plain + d, cross + d * norm

        zero = jnp.zeros((W, C), F32)
        plain, cross = lax.fori_loop(0, H, dnorm, (zero, zero), unroll=2)
        sums.append((jnp.sum(plain, axis=0, keepdims=True), jnp.sum(cross, axis=0, keepdims=True)))
    gat3[0][w.me] = jnp.concatenate([a for a, _ in sums] + [b for _, b in sums], axis=0)
    sent3 = gather_start(w, *gat3)
    for cp in copies2:
        cp.wait()
    halo_unpack(sp, T, hal2[1], hal2[3])

    def act2(k, _):
        build_act(w, sp, k, st2, mod, ab2, k)
        return 0

    lax.fori_loop(0, T, act2, 0)
    gather_wait(w, *gat3, sent3)
    sums = jnp.sum(gat3[0][...], axis=0)
    means = jnp.dot(sums, group_matrix(), precision=HI, preferred_element_type=F32)
    means = means * (1.0 / (H * W * w.nd * GSIZE))

    chain2 = Chain(w, run.at[0], ch2, True)

    def through(i, _):
        rgv = rg[i]
        acc = None
        for k in range(T - 1, -1, -1):
            center, inv = st2[k : k + 1, :], st2[T + k : T + k + 1, :]
            plain, cross = means[k : k + 1, :], means[T + k : T + k + 1, :]
            norm = (sp[k, i + 1, 0:W, :] - center) * inv
            d = (dact[k, i] - plain - norm * cross) * inv
            t = cstate[k] * rgv + (cdrift[k] * rgv + d)
            acc = t if acc is None else acc + t
            run[k, i] = acc
        return 0

    for j in range(CH):
        lax.fori_loop(0, ROWS, lambda i, z, j=j: through(ROWS * j + i, z), 0)
        chain2.pair(2 * j).start()
        chain2.pair(2 * j + 1).start()

    def second(j, _):
        sweep(lambda k, j: sp[k, pl.ds(1 + ROWS * j, ROWS), 0:W, :], ab2, run2, j)
        return 0

    def weight2(d, _):
        wgrad(upt2, ab2, g, d, True)
        return 0

    n = jnp.clip(2 * chain2.x, 0, CH)
    m = jnp.where(chain2.x == chips - 1, DOTS, 0)
    loop_where(CH, lambda j: j < n, second)
    loop_where(DOTS, lambda d: d < m, weight2)
    chain2.steps()
    loop_where(CH, lambda j: j >= n, second)
    for j in range(CH):
        chain3.pair(j).start()
    store = pltpu.make_async_copy(run2, run_h, local.at[5])
    store.start()
    loop_where(DOTS, lambda d: d >= m, weight2)
    chain2.finish()
    chain3.some(0, CH, chain3.x == 0)

    for k in range(T):
        adj = chain2.off[...] + run[k + 1] if k + 1 < T else chain2.off[...]
        up = (cdrift[k] * adj).reshape(H * W, C).astype(BF16)
        upt1[:, k * H * W : (k + 1) * H * W] = up.T

    def pairs(h):
        return rcopy(g.at[:, 1 - c, h], ra.at[h], sa.at[h], qa.at[h], partner)

    done = []

    def go(cp):
        cp.start()
        done.append(cp)

    def weight1(d, _):
        wgrad(upt1, ab1, g, d, False)
        return 0

    per = s.shape[4]
    two = per // 2

    def add(h):
        pairs(h).wait_recv()

        def one(q, _):
            place = pl.ds(per * q, per)
            for x in range(chips):
                s[h, x, lax.div(q, nx), lax.rem(q, nx)] = g[x, c, h, place] + ra[h, x, place]
            return 0

        lax.fori_loop(0, w.nd, one, 0)

    def chips_first():
        for d in range(1, chips):
            q, dev = chip(d)
            go(rcopy(s.at[0, q], rf.at[xme], sf.at[d], qf.at[xme], dev))

    def chips_join():
        for d in range(1, chips):
            q, dev = chip(d)
            rcopy(rf.at[q], rf.at[q], sf.at[d], qf.at[q], dev).wait_recv()

        def one(i, _):
            acc = s[0, xme, i]
            for d in range(1, chips):
                acc += rf[lax.rem(xme + d, chips), i]
            sx[0, i] = acc
            return 0

        lax.fori_loop(0, ny, one, 0)

    def source(h):
        return (s.at[h], chips) if h else (sx, 1)

    def along(h):
        b = h * (nx + ny)
        src, n = source(h)
        for d in range(1, nx):
            q = lax.rem(w.x + d, nx)
            go(rcopy(src.at[:, :, q, 0:two], rz.at[h, w.x, 0:n], sb.at[b + d], qb.at[b + w.x], w.shift(0, d)))
        for d in range(1, ny):
            q = lax.rem(w.y + d, ny)
            b2 = b + nx
            go(rcopy(src.at[:, q, :, two:per], ry.at[h, w.y, 0:n], sb.at[b2 + d], qb.at[b2 + w.y], w.shift(d, 0)))

    def across(h):
        b = h * (nx + ny)
        src, n = source(h)
        for d in range(1, nx):
            q = lax.rem(w.x + d, nx)
            rcopy(rz.at[h, q, 0:n], rz.at[h, q, 0:n], sb.at[b + d], qb.at[b + q], partner).wait_recv()
        for d in range(1, ny):
            q = lax.rem(w.y + d, ny)
            b2 = b + nx
            rcopy(ry.at[h, q, 0:n], ry.at[h, q, 0:n], sb.at[b2 + d], qb.at[b2 + q], partner).wait_recv()

        def join(x, _):
            for i in range(ny):
                acc = src[x, i, w.x, 0:two]
                for d in range(1, nx):
                    acc += rz[h, lax.rem(w.x + d, nx), x, i]
                s1[h, 0, x, i] = acc
            for j in range(nx):
                acc = src[x, w.y, j, two:per]
                for d in range(1, ny):
                    acc += ry[h, lax.rem(w.y + d, ny), x, j]
                s1[h, 1, x, j] = acc
            return 0

        lax.fori_loop(0, n, join, 0)
        b = h * (nx + ny)
        for d in range(1, ny):
            q = lax.rem(w.y + d, ny)
            go(rcopy(s1.at[h, 0, 0:n, q], rz1.at[h, w.y, 0:n], sc_.at[b + d], qc.at[b + w.y], w.shift(d, 0)))
        for d in range(1, nx):
            q = lax.rem(w.x + d, nx)
            b2 = b + ny
            go(rcopy(s1.at[h, 1, 0:n, q], ry1.at[h, w.x, 0:n], sc_.at[b2 + d], qc.at[b2 + w.x], w.shift(0, d)))

    def chips_out(h):
        b = h * (nx + ny)
        n = source(h)[1]
        for d in range(1, ny):
            q = lax.rem(w.y + d, ny)
            rcopy(rz1.at[h, q, 0:n], rz1.at[h, q, 0:n], sc_.at[b + d], qc.at[b + q], partner).wait_recv()
        for d in range(1, nx):
            q = lax.rem(w.x + d, nx)
            b2 = b + ny
            rcopy(ry1.at[h, q, 0:n], ry1.at[h, q, 0:n], sc_.at[b2 + d], qc.at[b2 + q], partner).wait_recv()
        for x in range(n):
            acc = s1[h, 0, x, w.y]
            for d in range(1, ny):
                acc += rz1[h, lax.rem(w.y + d, ny), x]
            s2[h, x, 0:two] = acc
            acc = s1[h, 1, x, w.x]
            for d in range(1, nx):
                acc += ry1[h, lax.rem(w.x + d, nx), x]
            s2[h, x, two:per] = acc
        for d in range(1, chips if h else 1):
            q, dev = chip(d)
            go(rcopy(s2.at[h, q], rx.at[h, xme], sd.at[h * chips + d], qd.at[h * chips + xme], dev))

    def spread(h):
        for d in range(1, chips if h else 1):
            q, dev = chip(d)
            rcopy(rx.at[h, q], rx.at[h, q], sd.at[h * chips + d], qd.at[h * chips + q], dev).wait_recv()
        acc = s2[h, xme] if h else s2[0, 0]
        for d in range(1, chips if h else 1):
            acc += rx[h, lax.rem(xme + d, chips)]
        fin[h, w.me] = acc
        b = pl.ds(h * w.nd, w.nd)
        return gather_start(w, fin.at[h], se.at[b], qe.at[b])

    for h in range(PARTS):
        lax.fori_loop(PART * h, PART * h + PART, weight1, 0)
        pairs(h).start()
        if h == 2:
            add(0)
            chips_first()
        if h == 3:
            add(1)
            along(1)
    for h in (2, 3):
        add(h)
        along(h)
    chain3.some(0, CH, chain3.x == 1)
    across(1)
    chips_join()
    along(0)
    across(2)
    chips_out(1)
    across(3)
    chain3.some(0, CH, chain3.x == 2)
    across(0)
    sent = [None, spread(1)]
    chips_out(2)
    chips_out(3)
    chips_out(0)
    sent[0] = spread(0)
    sent += [spread(2), spread(3)]
    chain3.some(0, CH, chain3.x == chips - 1)
    chain3.finish()
    store2 = pltpu.make_async_copy(chain3.off, off_h, local.at[6])
    store2.start()
    for h in range(PARTS):
        b = pl.ds(h * w.nd, w.nd)
        gather_wait(w, fin.at[h], se.at[b], qe.at[b], sent[h])
    for r in range(3):
        cols = []
        for l in range(8):
            d = 4 * r + l // 2
            first_tile = 10 * (d % PART) + 5 * (l % 2)
            tiles = [fin[d // PART, t // per, t % per] for t in range(first_tile, first_tile + 5)]
            cols.append(jnp.concatenate(tiles, axis=0))
        whole = jnp.concatenate(cols, axis=1)
        for q in range(3):
            out[r, q, :, 0:256] = whole[:, 256 * q : 256 * q + 256]
            out[r, q, :, 256:C] = whole[:, 768 + 64 * q : 832 + 64 * q]
    store.wait()
    store2.wait()
    for h in range(PARTS):
        pairs(h).wait_send()
    for cp in done:
        cp.wait_send()


def shards(dims, latent, noise, coef_state, coef_drift, coef_noise, step_index, table, gain, weight, rg):
    nt, ny, nx = dims
    nd = ny * nx
    chips = nt // 2
    per = TILES // nd
    half = per // 2
    dma = pltpu.SemaphoreType.DMA
    vmem = pltpu.VMEM
    field = (T, H, W, C)
    packed = (T, HP, W, AW)
    scratch = [
        vmem((2, HP, PW, C), F32),
        vmem((T, HP, PW, C), F32),
        vmem(field, F32),
        vmem(field, F32),
        vmem(field, F32),
        vmem(packed, BF16),
        vmem(packed, BF16),
        vmem(packed, BF16),
        vmem((3, AW, C), BF16),
        vmem((3, AW, C), BF16),
        vmem((T, C), F32),
        vmem((2 * T, C), F32),
        vmem((2 * T, C), F32),
        vmem((C, T * H * W), BF16),
        vmem((C, T * H * W), BF16),
    ]
    scratch += halo_scratch(2) + halo_scratch(T)
    scratch += gather_scratch(nd) * 3 + chain_scratch(2 * CH) * 2 + chain_scratch(CH)
    scratch += [
        vmem((chips, 2, PARTS, TILES, 8, 128), F32),
        vmem((PARTS, chips, TILES, 8, 128), F32),
        vmem((PARTS, chips, ny, nx, per, 8, 128), F32),
        vmem((PARTS, ny, chips, nx, half, 8, 128), F32),
        vmem((PARTS, nx, chips, ny, half, 8, 128), F32),
        vmem((PARTS, 2, chips, max(nx, ny), half, 8, 128), F32),
        vmem((PARTS, ny, chips, half, 8, 128), F32),
        vmem((PARTS, nx, chips, half, 8, 128), F32),
        vmem((PARTS, chips, per, 8, 128), F32),
        vmem((PARTS, chips, per, 8, 128), F32),
        vmem((PARTS, nd, per, 8, 128), F32),
        vmem(noise.shape, BF16),
        vmem(weight.shape, BF16),
        vmem(table.shape[::-1], F32),
        vmem((H, W, C), F32),
        vmem((H, W, C), F32),
        vmem((1, ny, nx, per, 8, 128), F32),
        vmem((chips, ny, nx, per, 8, 128), F32),
        dma((7,)),
    ]
    for count in (1, nx + ny, nx + ny, chips, nd):
        scratch += [dma((PARTS * count,)), dma((PARTS * count,))]
    scratch += [dma((chips,)), dma((chips,))]
    run, off, out = pl.pallas_call(
        functools.partial(k_all, dims),
        out_shape=(
            jax.ShapeDtypeStruct(field, F32),
            jax.ShapeDtypeStruct((H, W, C), F32),
            jax.ShapeDtypeStruct((3, 3, C // nt, C), F32),
        ),
        in_specs=[SM] * 4 + [ANY] * 5 + [VM],
        out_specs=(ANY, ANY, VM),
        scratch_shapes=scratch,
        compiler_params=pltpu.CompilerParams(
            vmem_limit_bytes=VLIM, collective_id=0, has_side_effects=True
        ),
        name="picard",
    )(step_index, coef_state, coef_drift, coef_noise, latent, rg, noise, weight, table.T, gain)
    traj = latent[None] + (off[None] + run)
    return traj, jnp.transpose(out, (0, 1, 3, 2))


def solution(mesh):
    dims = (mesh.shape["tm"], mesh.shape["sy"], mesh.shape["sx"])
    tile = P("sy", "sx", None)
    full = P("tm", "sy", "sx", None)
    step = P("tm")
    return jax.shard_map(
        functools.partial(shards, dims),
        mesh=mesh,
        in_specs=(tile, full, step, step, step, step, P(), P(), P(), tile),
        out_specs=(full, P(None, None, None, "tm")),
        check_vma=False,
    )
```
